32 devices in a mesh: row: 8 (over z, y), col: 4 (over x, core).
Axes of the slice: x: 2, y: 2, z: 4, core: 2. Of those that a mesh axis runs over, the one named last changes fastest.
Arguments:
- panel: bfloat16 [2, 8, 512, 4, 512], P(None, 'row', None, 'col'), may hold values from -0.25 to 0.25
- rhs: float32 [2, 8, 512, 2048], P(None, 'row', None, 'col'), may hold values from -6 to 6
- inverse: bfloat16 [4, 512, 512], replicated, as said below
Outputs:
- solved: float32 [4, 512, 2048], P(None, None, 'col')
- remainder: float32 [2, 8, 512, 2048], P(None, 'row', None, 'col')
The draws below stay inside these ranges and needn't reach their ends.
Inputs may be any that keep to these rules, and one draw needn't show every extreme that they name: Each block of inverse is lower triangular with a positive diagonal.
All inputs are finite; a program needn't handle non-finite values.
Results may differ from the reference program's by a relative error of at most 0.008.
Values may be sent and summed in bfloat16 or wider, within the bound.
A program may use at most 128 MiB of HBM per device.

```python
import math
import jax
import jax.numpy as jnp

B = 512
NRHS = 2048
RB = 2
STEPS = 4
OFF = 4
NB = 16
N_ROW = 8


def draw_inverse(key, part):
    first, second = jax.random.split(jax.random.fold_in(key, 7), 2)
    diagonal = jax.random.uniform(first, (STEPS, B), minval=0.6, maxval=1.4)
    spread = jax.random.normal(second, (STEPS, B, B)) * (0.7 / math.sqrt(B))
    lower = jnp.tril(spread, -1) + diagonal[:, :, None] * jnp.eye(B, dtype=jnp.float32)[None]
    return lower.astype(jnp.bfloat16)


def shard_levels(rng, shape, cuts, smallest, top_value):
    gain, own = 1.0, jax.random.fold_in(rng, 6)
    for dim, blocks in cuts:
        heights = jnp.exp(jax.random.uniform(jax.random.fold_in(own, dim), (blocks,), jnp.float32, smallest / len(cuts), top_value / len(cuts)))
        gain = gain * jnp.repeat(heights, shape[dim] // blocks).reshape([-1 if axis == dim else 1 for axis in range(len(shape))])
    return gain


def gaussian(stream_key, shape, scale, limit, pieces=(), kind=jnp.bfloat16):
    factor_of = shard_levels(stream_key, shape, pieces, -0.22, 0.18) if pieces else 1.0
    entries = jax.random.normal(stream_key, shape, jnp.float32) * scale * factor_of
    return jnp.minimum(jnp.maximum(entries, -limit), limit).astype(kind)


def setup_inputs(seed: int = 0) -> dict:
    splits = jax.random.split(jax.random.key(seed), 4)
    return {
        "panel": gaussian(splits[0], (RB, N_ROW, B, STEPS, B), (B * STEPS // 4) ** -0.5, 0.25, ((1, 8), (3, 4))),
        "rhs": gaussian(splits[1], (RB, N_ROW, B, NRHS), 1.0, 6.0, ((1, 8), (3, 4)), jnp.float32),
        "inverse": draw_inverse(jax.random.fold_in(splits[3], 71), 0),
    }


def reference(panel, rhs, inverse):
    blocks = panel.reshape(NB, B, STEPS, B)
    right = rhs.reshape(NB, B, NRHS)
    solved_list = []
    low_list = []
    for k in range(STEPS):
        base = right[OFF + k]
        if k > 0:
            left = blocks[OFF + k, :, :k, :].reshape(B, k * B)
            lower = jnp.stack(low_list, axis=0).reshape(k * B, NRHS)
            base = base - jnp.dot(left, lower, preferred_element_type=jnp.float32)
        fresh = jnp.dot(inverse[k], base.astype(jnp.bfloat16), preferred_element_type=jnp.float32)
        solved_list.append(fresh)
        low_list.append(fresh.astype(jnp.bfloat16))
    solved = jnp.stack(solved_list, axis=0)
    lower_all = jnp.stack(low_list, axis=0).reshape(STEPS * B, NRHS)
    block_rows = jnp.arange(NB, dtype=jnp.int32)
    block_cols = jnp.arange(STEPS, dtype=jnp.int32)
    keep = (block_cols[None, :] + OFF < block_rows[:, None]).astype(jnp.bfloat16)
    masked = blocks * keep[:, None, :, None]
    update = jnp.dot(masked.reshape(NB * B, STEPS * B), lower_all, preferred_element_type=jnp.float32)
    remainder = right - update.reshape(NB, B, NRHS)
    return solved, remainder.reshape(RB, N_ROW, B, NRHS)
```

```python
import functools

import jax
import jax.numpy as jnp
from jax import lax
from jax.experimental import pallas as pl
from jax.experimental.pallas import tpu as pltpu
from jax.sharding import PartitionSpec as P

MESH = pl.DeviceIdType.MESH


def kernel(
    n_rows, n_cols, steps, panel, rhs, inverse, low_out, rem_out,
    low, acc, inv, lower,
    load_sem, own_sem, inv_sem, low_sem, rem_sem, send_sem, recv_sem, psend_sem, precv_sem,
):
    rb = acc.shape[0]
    chunks, width = acc.shape[1], acc.shape[3]
    offset = n_rows - steps
    levels = n_rows // 2
    bits = [1 << b for b in reversed(range(n_cols.bit_length() - 1))]
    row, col = lax.axis_index("row"), lax.axis_index("col")
    level, side = row // 2, row % 2
    mine = row - offset
    inv_index = jnp.maximum(mine, 0)

    def flip(bit):
        return col + bit - 2 * bit * ((col // bit) % 2)

    targets = (row + 1 - 2 * side, row - 2, row + 2)
    exists = (level >= 0, level > 0, level < levels - 1)

    def columns(t):
        return pl.ds(pl.multiple_of(t * width, width), width)

    def load(q, t):
        return pltpu.make_async_copy(rhs.at[q, :, columns(t)], acc.at[q, t], load_sem.at[q, t])

    def load_own(q):
        return pltpu.make_async_copy(panel.at[q], lower.at[q, col], own_sem.at[q])

    load_inv = pltpu.make_async_copy(inverse.at[inv_index], inv, inv_sem)

    def store_low(k, t):
        return pltpu.make_async_copy(low.at[k, t], low_out.at[k, :, columns(t)], low_sem.at[k, t])

    def store_rem(q, t):
        return pltpu.make_async_copy(acc.at[q, t], rem_out.at[q, :, columns(t)], rem_sem.at[q, t])

    def send_low(way, k, t):
        return pltpu.make_async_remote_copy(
            src_ref=low.at[k, t], dst_ref=low.at[k, t],
            send_sem=send_sem.at[way, k, t], recv_sem=recv_sem.at[k, t],
            device_id={"row": targets[way]}, device_id_type=MESH,
        )

    def goes(way, k):
        home = (offset + k) // 2
        same = k % 2 == side
        if way == 0:
            return same
        if way == 1:
            return same & (level > 0) & (level <= home)
        return same & (level < levels - 1) & (level >= home)

    def forward(k, t):
        for way in range(3):
            @pl.when(goes(way, k))
            def _():
                send_low(way, k, t).start()

    def send_block(q, j, b):
        return pltpu.make_async_remote_copy(
            src_ref=lower.at[q, j], dst_ref=lower.at[q, j],
            send_sem=psend_sem.at[q, j, b], recv_sem=precv_sem.at[q, j],
            device_id={"col": flip(bits[b])}, device_id_type=MESH,
        )

    def send_own(q):
        load_own(q).wait()
        for b in range(len(bits)):
            send_block(q, col, b).start()

    def passes(j, b):
        return (col % (2 * bits[b])) == (j % (2 * bits[b]))

    def receive_block(q, j):
        @pl.when(col != j)
        def _():
            send_block(q, j, 0).wait_recv()
            for b in range(len(bits)):
                @pl.when(passes(j, b))
                def _():
                    send_block(q, j, b).start()

    @pl.when(mine >= 0)
    def _():
        load_inv.start()

    @pl.loop(0, chunks)
    def _(t):
        load(0, t).start()

    for q in range(rb):
        load_own(q).start()
    for q in range(1, rb):
        @pl.loop(0, chunks)
        def _(t):
            load(q, t).start()

    barrier = pltpu.get_barrier_semaphore()
    for way in range(3):
        @pl.when(exists[way])
        def _():
            pl.semaphore_signal(barrier, inc=1, device_id={"row": targets[way]}, device_id_type=MESH)
    for bit in bits:
        pl.semaphore_signal(barrier, inc=1, device_id={"col": flip(bit)}, device_id_type=MESH)
    pl.semaphore_wait(
        barrier,
        1 + len(bits) + jnp.minimum(level, 1) + jnp.minimum(levels - 1 - level, 1),
    )

    @pl.when(mine > col)
    def _():
        send_own(0)

    @pl.when(mine <= col)
    def _():
        load_own(0).wait()

    def send_later():
        for q in range(1, rb):
            send_own(q)

    @pl.when(mine < 1)
    def _():
        send_later()

    @pl.loop(0, chunks)
    def _(t):
        load(0, t).wait()

    def produce(t):
        @pl.loop(0, inv_index)
        def _(j):
            acc[0, t] -= jnp.dot(lower[0, j], low[j, t], preferred_element_type=jnp.float32)

        low[inv_index, t] = jnp.dot(
            inv[...], acc[0, t].astype(jnp.bfloat16), preferred_element_type=jnp.float32
        ).astype(jnp.bfloat16)
        forward(inv_index, t)
        store_low(inv_index, t).start()
        store_rem(0, t).start()

    @pl.when(mine >= 0)
    def _():
        load_inv.wait()

    @pl.when(mine == 0)
    def _():
        @pl.loop(0, chunks)
        def _(t):
            produce(t)

    @pl.when(mine < 0)
    def _():
        @pl.loop(0, chunks)
        def _(t):
            store_rem(0, t).start()

    gather_at = (steps - 1 - side) * chunks
    last = steps - 1 - side

    @pl.loop(0, steps * chunks)
    def _(e):
        inner = e % (2 * chunks)
        k_plain, t_plain = e // chunks, e % chunks
        k_pair, t_pair = 2 * (e // (2 * chunks)) + 1 - inner % 2, inner // 2
        k = k_plain + side * (k_pair - k_plain)
        t = t_plain + side * (t_pair - t_plain)

        @pl.when((e == chunks) & (mine >= 1))
        def _():
            send_later()

        @pl.when(e == gather_at)
        def _():
            for q in range(1, rb):
                @pl.loop(0, n_cols)
                def _(j):
                    receive_block(q, j)

                @pl.loop(0, chunks)
                def _(u):
                    load(q, u).wait()

        @pl.when(mine != k)
        def _():
            send_low(0, k, t).wait_recv()
            forward(k, t)
            store_low(k, t).start()

        @pl.when(mine == k + 1)
        def _():
            @pl.when(t == 0)
            def _():
                @pl.loop(0, inv_index)
                def _(j):
                    receive_block(0, j)

            produce(t)

        @pl.when(k == last)
        def _():
            for q in range(1, rb):
                for j in range(steps):
                    acc[q, t] -= jnp.dot(
                        lower[q, j], low[j, t], preferred_element_type=jnp.float32
                    )
                store_rem(q, t).start()

    @pl.loop(0, steps * chunks)
    def _(e):
        k, t = e // chunks, e % chunks
        store_low(k, t).wait()
        for way in range(3):
            @pl.when(goes(way, k))
            def _():
                send_low(way, k, t).wait_send()

    for q in range(rb):
        @pl.loop(0, chunks)
        def _(t):
            store_rem(q, t).wait()

        @pl.loop(0, n_cols)
        def _(j):
            used = mine > j if q == 0 else mine >= -n_rows
            for b in range(len(bits)):
                @pl.when(used & passes(j, b))
                def _():
                    send_block(q, j, b).wait_send()


def on_device(n_rows, n_cols, panel, rhs, inverse):
    rb, block = panel.shape[0], panel.shape[2]
    cols = rhs.shape[3]
    steps = inverse.shape[0]
    assert panel.shape[3] == 1 and n_cols == steps
    assert n_rows % 2 == 0 and steps % 2 == 0 and n_cols & (n_cols - 1) == 0
    width = 128 if cols % 128 == 0 else cols
    chunks = cols // width
    bits = n_cols.bit_length() - 1
    dma = pltpu.SemaphoreType.DMA
    low, remainder = pl.pallas_call(
        functools.partial(kernel, n_rows, n_cols, steps),
        out_shape=(
            jax.ShapeDtypeStruct((steps, block, cols), jnp.bfloat16),
            jax.ShapeDtypeStruct((rb, block, cols), jnp.float32),
        ),
        in_specs=[pl.BlockSpec(memory_space=pl.ANY)] * 3,
        out_specs=(pl.BlockSpec(memory_space=pl.ANY),) * 2,
        scratch_shapes=[
            pltpu.VMEM((steps, chunks, block, width), jnp.bfloat16),
            pltpu.VMEM((rb, chunks, block, width), jnp.float32),
            pltpu.VMEM((block, block), jnp.bfloat16),
            pltpu.VMEM((rb, steps, block, block), jnp.bfloat16),
            dma((rb, chunks)),
            dma((rb,)),
            dma,
            dma((steps, chunks)),
            dma((rb, chunks)),
            dma((3, steps, chunks)),
            dma((steps, chunks)),
            dma((rb, n_cols, bits)),
            dma((rb, n_cols)),
        ],
        compiler_params=pltpu.CompilerParams(
            collective_id=0, has_side_effects=True, vmem_limit_bytes=40 * 2**20
        ),
    )(panel.reshape(rb, block, block), rhs.reshape(rb, block, cols), inverse)
    return low.astype(jnp.float32), remainder.reshape(rhs.shape)


def solution(mesh):
    placed = (P(None, "row", None, "col", None), P(None, "row", None, "col"), P())
    return jax.shard_map(
        functools.partial(on_device, mesh.shape["row"], mesh.shape["col"]),
        mesh=mesh,
        in_specs=placed,
        out_specs=(P(None, None, "col"), P(None, "row", None, "col")),
        check_vma=False,
    )
```

```python
import functools

import jax
import jax.numpy as jnp
from jax import lax
from jax.experimental import pallas as pl
from jax.experimental.pallas import tpu as pltpu
from jax.sharding import PartitionSpec as P

MESH = pl.DeviceIdType.MESH


def kernel(
    n_rows, n_cols, steps, panel, rhs, inverse, low_out, rem_out,
    low, natural, base_ref, acc, inv, lower,
    load_sem, own_sem, inv_sem, low_sem, rem_sem, send_sem, recv_sem, psend_sem, precv_sem,
):
    rb = acc.shape[0]
    tiles, block, width = acc.shape[1:]
    chunks = low.shape[1]
    fold = chunks // tiles
    part, height = width // fold, block // fold
    offset = n_rows - steps
    levels = n_rows // 2
    bits = [1 << b for b in reversed(range(n_cols.bit_length() - 1))]
    row, col = lax.axis_index("row"), lax.axis_index("col")
    level, side = row // 2, row % 2
    mine = row - offset
    inv_index = jnp.maximum(mine, 0)

    def flip(bit):
        return col + bit - 2 * bit * ((col // bit) % 2)

    targets = (row + 1 - 2 * side, row - 2, row + 2)
    exists = (level >= 0, level > 0, level < levels - 1)

    def columns(t):
        return pl.ds(pl.multiple_of(t * width, width), width)

    def load(q, t):
        return pltpu.make_async_copy(rhs.at[q, :, columns(t)], acc.at[q, t], load_sem.at[q, t])

    def load_own(q):
        return pltpu.make_async_copy(panel.at[q], lower.at[q, col], own_sem.at[q])

    load_inv = pltpu.make_async_copy(inverse.at[inv_index], inv, inv_sem)

    def store_low(k, t):
        return pltpu.make_async_copy(natural.at[k, t], low_out.at[k, :, columns(t)], low_sem.at[k])

    def store_rem(q, t):
        return pltpu.make_async_copy(acc.at[q, t], rem_out.at[q, :, columns(t)], rem_sem.at[q])

    def send_low(way, k, t):
        return pltpu.make_async_remote_copy(
            src_ref=low.at[k, t], dst_ref=low.at[k, t],
            send_sem=send_sem.at[way, k], recv_sem=recv_sem.at[k, t],
            device_id={"row": targets[way]}, device_id_type=MESH,
        )

    def goes(way, k):
        home = (offset + k) // 2
        same = k % 2 == side
        if way == 0:
            return same
        if way == 1:
            return same & (level > 0) & (level <= home)
        return same & (level < levels - 1) & (level >= home)

    def forward(k, t):
        for way in range(3):
            @pl.when(goes(way, k))
            def _():
                send_low(way, k, t).start()

    lane = lax.broadcasted_iota(jnp.int32, (height, width), 1) // part

    def turn(x, shift):
        return pltpu.roll(x, lax.rem(shift + width, width), 1)

    def spread(p):
        wide = p.astype(jnp.float32)
        return jnp.concatenate(
            [wide] + [pltpu.roll(wide, width - g * part, 1) for g in range(1, fold)], axis=0
        ).astype(jnp.bfloat16)

    def pack(x):
        out = x[:height]
        for g in range(1, fold):
            moved = pltpu.roll(x[g * height : (g + 1) * height], g * part, 1)
            out = jnp.where(lane == g, moved, out)
        return out.astype(jnp.bfloat16)

    def unpack(k, tile):
        held = [low[k, tile * fold + h].astype(jnp.float32) for h in range(fold)]
        for g in range(fold):
            out = held[0] if g == 0 else pltpu.roll(held[0], width - g * part, 1)
            for h in range(1, fold):
                shift = (h - g) * part % width
                moved = held[h] if shift == 0 else pltpu.roll(held[h], shift, 1)
                out = jnp.where(lane == h, moved, out)
            natural[k, tile, pl.ds(g * height, height), :] = out.astype(jnp.bfloat16)
        store_low(k, tile).start()

    def send_block(q, j, b):
        return pltpu.make_async_remote_copy(
            src_ref=lower.at[q, j], dst_ref=lower.at[q, j],
            send_sem=psend_sem.at[q, j, b], recv_sem=precv_sem.at[q, j],
            device_id={"col": flip(bits[b])}, device_id_type=MESH,
        )

    def send_own(q):
        load_own(q).wait()
        for b in range(len(bits)):
            send_block(q, col, b).start()

    def passes(j, b):
        return (col % (2 * bits[b])) == (j % (2 * bits[b]))

    def receive_block(q, j):
        @pl.when(col != j)
        def _():
            send_block(q, j, 0).wait_recv()
            for b in range(len(bits)):
                @pl.when(passes(j, b))
                def _():
                    send_block(q, j, b).start()

    @pl.when(mine >= 0)
    def _():
        load_inv.start()

    @pl.loop(0, tiles)
    def _(t):
        load(0, t).start()

    for q in range(rb):
        load_own(q).start()
    for q in range(1, rb):
        @pl.loop(0, tiles)
        def _(t):
            load(q, t).start()

    barrier = pltpu.get_barrier_semaphore()
    for way in range(3):
        @pl.when(exists[way])
        def _():
            pl.semaphore_signal(barrier, inc=1, device_id={"row": targets[way]}, device_id_type=MESH)
    for bit in bits:
        pl.semaphore_signal(barrier, inc=1, device_id={"col": flip(bit)}, device_id_type=MESH)
    pl.semaphore_wait(
        barrier,
        1 + len(bits) + jnp.minimum(level, 1) + jnp.minimum(levels - 1 - level, 1),
    )

    @pl.when(mine > col)
    def _():
        send_own(0)

    @pl.when(mine <= col)
    def _():
        load_own(0).wait()

    def send_later():
        for q in range(1, rb):
            send_own(q)

    @pl.when(mine < 1)
    def _():
        send_later()

    @pl.loop(0, tiles)
    def _(t):
        load(0, t).wait()

    def produce(t):
        tile, h = t // fold, t % fold
        base_ref[...] = turn(acc[0, tile], -h * part)

        @pl.loop(0, inv_index)
        def _(j):
            base_ref[...] -= jnp.dot(
                lower[0, j], spread(low[j, t]), preferred_element_type=jnp.float32
            )

        base = base_ref[...]
        low[inv_index, t] = pack(
            jnp.dot(inv[...], base.astype(jnp.bfloat16), preferred_element_type=jnp.float32)
        )
        forward(inv_index, t)
        group = lax.broadcasted_iota(jnp.int32, (block, width), 1) // part
        acc[0, tile] = jnp.where(group == h, turn(base, h * part), acc[0, tile])

        @pl.when(h == fold - 1)
        def _():
            store_rem(0, tile).start()
            unpack(inv_index, tile)

    @pl.when(mine >= 0)
    def _():
        load_inv.wait()

    @pl.when(mine == 0)
    def _():
        @pl.loop(0, chunks)
        def _(t):
            produce(t)

    @pl.when(mine < 0)
    def _():
        @pl.loop(0, tiles)
        def _(t):
            store_rem(0, t).start()

    gather_at = (steps - 1 - side) * chunks
    last = steps - 1 - side

    @pl.loop(0, steps * chunks)
    def _(e):
        inner = e % (2 * chunks)
        k_plain, t_plain = e // chunks, e % chunks
        k_pair, t_pair = 2 * (e // (2 * chunks)) + 1 - inner % 2, inner // 2
        k = k_plain + side * (k_pair - k_plain)
        t = t_plain + side * (t_pair - t_plain)

        @pl.when((e == chunks) & (mine >= 1))
        def _():
            send_later()

        @pl.when(e == gather_at)
        def _():
            for q in range(1, rb):
                @pl.loop(0, n_cols)
                def _(j):
                    receive_block(q, j)

                @pl.loop(0, tiles)
                def _(u):
                    load(q, u).wait()

        @pl.when(mine != k)
        def _():
            send_low(0, k, t).wait_recv()
            forward(k, t)

            @pl.when(t % fold == fold - 1)
            def _():
                unpack(k, t // fold)

        @pl.when(mine == k + 1)
        def _():
            @pl.when(t == 0)
            def _():
                @pl.loop(0, inv_index)
                def _(j):
                    receive_block(0, j)

            produce(t)

        @pl.when((k == last) & (t % fold == fold - 1))
        def _():
            tile = t // fold
            for q in range(1, rb):
                for j in range(steps):
                    acc[q, tile] -= jnp.dot(
                        lower[q, j], natural[j, tile], preferred_element_type=jnp.float32
                    )
                store_rem(q, tile).start()

    for k in range(steps):
        for way in range(3):
            @pl.when(goes(way, k))
            def _():
                pltpu.make_async_remote_copy(
                    src_ref=low.at[k], dst_ref=low.at[k],
                    send_sem=send_sem.at[way, k], recv_sem=recv_sem.at[k, 0],
                    device_id={"row": targets[way]}, device_id_type=MESH,
                ).wait_send()
    for q in range(rb):
        for j in range(n_cols):
            used = mine > j if q == 0 else mine >= -n_rows
            for b in range(len(bits)):
                @pl.when(used & passes(j, b))
                def _():
                    send_block(q, j, b).wait_send()
    for k in range(steps):
        pltpu.make_async_copy(natural.at[k], natural.at[k], low_sem.at[k]).wait()
    for q in range(rb):
        pltpu.make_async_copy(acc.at[q], acc.at[q], rem_sem.at[q]).wait()


def on_device(n_rows, n_cols, panel, rhs, inverse):
    rb, block = panel.shape[0], panel.shape[2]
    cols = rhs.shape[3]
    steps = inverse.shape[0]
    assert panel.shape[3] == 1 and n_cols == steps
    assert n_rows % 2 == 0 and steps % 2 == 0 and n_cols & (n_cols - 1) == 0
    width = 128 if cols % 128 == 0 else cols
    tiles = cols // width
    fold = 2
    bits = n_cols.bit_length() - 1
    dma = pltpu.SemaphoreType.DMA
    low, remainder = pl.pallas_call(
        functools.partial(kernel, n_rows, n_cols, steps),
        out_shape=(
            jax.ShapeDtypeStruct((steps, block, cols), jnp.bfloat16),
            jax.ShapeDtypeStruct((rb, block, cols), jnp.float32),
        ),
        in_specs=[pl.BlockSpec(memory_space=pl.ANY)] * 3,
        out_specs=(pl.BlockSpec(memory_space=pl.ANY),) * 2,
        scratch_shapes=[
            pltpu.VMEM((steps, tiles * fold, block // fold, width), jnp.bfloat16),
            pltpu.VMEM((steps, tiles, block, width), jnp.bfloat16),
            pltpu.VMEM((block, width), jnp.float32),
            pltpu.VMEM((rb, tiles, block, width), jnp.float32),
            pltpu.VMEM((block, block), jnp.bfloat16),
            pltpu.VMEM((rb, steps, block, block), jnp.bfloat16),
            dma((rb, tiles)),
            dma((rb,)),
            dma,
            dma((steps,)),
            dma((rb,)),
            dma((3, steps)),
            dma((steps, tiles * fold)),
            dma((rb, n_cols, bits)),
            dma((rb, n_cols)),
        ],
        compiler_params=pltpu.CompilerParams(
            collective_id=0, has_side_effects=True, vmem_limit_bytes=60 * 2**20
        ),
    )(panel.reshape(rb, block, block), rhs.reshape(rb, block, cols), inverse)
    return low.astype(jnp.float32), remainder.reshape(rhs.shape)


def solution(mesh):
    placed = (P(None, "row", None, "col", None), P(None, "row", None, "col"), P())
    return jax.shard_map(
        functools.partial(on_device, mesh.shape["row"], mesh.shape["col"]),
        mesh=mesh,
        in_specs=placed,
        out_specs=(P(None, None, "col"), P(None, "row", None, "col")),
        check_vma=False,
    )
```

```python
import functools

import jax
import jax.numpy as jnp
from jax import lax
from jax.experimental import pallas as pl
from jax.experimental.pallas import tpu as pltpu
from jax.sharding import PartitionSpec as P

MESH = pl.DeviceIdType.MESH


def kernel(
    n_rows, n_cols, steps, panel, rhs, inverse, low_out, rem_out,
    low, natural, acc, inv, lower,
    load_sem, own_sem, inv_sem, low_sem, rem_sem, send_sem, recv_sem, psend_sem, precv_sem,
):
    rb = acc.shape[0]
    tiles, block, width = acc.shape[1:]
    chunks = low.shape[1]
    fold = chunks // tiles
    part, height = width // fold, block // fold
    offset = n_rows - steps
    levels = n_rows // 2
    bits = [1 << b for b in reversed(range(n_cols.bit_length() - 1))]
    row, col = lax.axis_index("row"), lax.axis_index("col")
    level, side = row // 2, row % 2
    mine = row - offset
    inv_index = jnp.maximum(mine, 0)

    def flip(bit):
        return col + bit - 2 * bit * ((col // bit) % 2)

    targets = (row + 1 - 2 * side, row - 2, row + 2)
    exists = (level >= 0, level > 0, level < levels - 1)

    def columns(t):
        return pl.ds(pl.multiple_of(t * width, width), width)

    def load(q, t):
        return pltpu.make_async_copy(rhs.at[q, :, columns(t)], acc.at[q, t], load_sem.at[q, t])

    def load_own(q):
        return pltpu.make_async_copy(panel.at[q], lower.at[q, col], own_sem.at[q])

    load_inv = pltpu.make_async_copy(inverse.at[inv_index], inv, inv_sem)

    def store_low(k, t):
        return pltpu.make_async_copy(natural.at[k, t], low_out.at[k, :, columns(t)], low_sem.at[k])

    def store_rem(q, t):
        return pltpu.make_async_copy(acc.at[q, t], rem_out.at[q, :, columns(t)], rem_sem.at[q])

    def send_low(way, k, t):
        return pltpu.make_async_remote_copy(
            src_ref=low.at[k, t], dst_ref=low.at[k, t],
            send_sem=send_sem.at[way, k], recv_sem=recv_sem.at[k, t],
            device_id={"row": targets[way]}, device_id_type=MESH,
        )

    def goes(way, k):
        home = (offset + k) // 2
        same = k % 2 == side
        if way == 0:
            return same
        if way == 1:
            return same & (level > 0) & (level <= home)
        return same & (level < levels - 1) & (level >= home)

    def forward(k, t):
        for way in range(3):
            @pl.when(goes(way, k))
            def _():
                send_low(way, k, t).start()

    lane = lax.broadcasted_iota(jnp.int32, (height, width), 1) // part

    def turn(x, shift):
        return pltpu.roll(x, lax.rem(shift + width, width), 1)

    def spread(p):
        wide = p.astype(jnp.float32)
        return jnp.concatenate(
            [wide] + [pltpu.roll(wide, width - g * part, 1) for g in range(1, fold)], axis=0
        ).astype(jnp.bfloat16)

    def pack(x):
        out = x[:height]
        for g in range(1, fold):
            moved = pltpu.roll(x[g * height : (g + 1) * height], g * part, 1)
            out = jnp.where(lane == g, moved, out)
        return out.astype(jnp.bfloat16)

    def unpack(k, tile):
        held = [low[k, tile * fold + h].astype(jnp.float32) for h in range(fold)]
        for g in range(fold):
            out = held[0] if g == 0 else pltpu.roll(held[0], width - g * part, 1)
            for h in range(1, fold):
                shift = (h - g) * part % width
                moved = held[h] if shift == 0 else pltpu.roll(held[h], shift, 1)
                out = jnp.where(lane == h, moved, out)
            natural[k, tile, pl.ds(g * height, height), :] = out.astype(jnp.bfloat16)
        store_low(k, tile).start()

    def send_block(q, j, b):
        return pltpu.make_async_remote_copy(
            src_ref=lower.at[q, j], dst_ref=lower.at[q, j],
            send_sem=psend_sem.at[q, j, b], recv_sem=precv_sem.at[q, j],
            device_id={"col": flip(bits[b])}, device_id_type=MESH,
        )

    def send_own(q):
        load_own(q).wait()
        for b in range(len(bits)):
            send_block(q, col, b).start()

    def passes(j, b):
        return (col % (2 * bits[b])) == (j % (2 * bits[b]))

    def receive_block(q, j):
        @pl.when(col != j)
        def _():
            send_block(q, j, 0).wait_recv()
            for b in range(len(bits)):
                @pl.when(passes(j, b))
                def _():
                    send_block(q, j, b).start()

    @pl.when(mine >= 0)
    def _():
        load_inv.start()

    @pl.loop(0, tiles)
    def _(t):
        load(0, t).start()

    for q in range(rb):
        load_own(q).start()
    for q in range(1, rb):
        @pl.loop(0, tiles)
        def _(t):
            load(q, t).start()

    barrier = pltpu.get_barrier_semaphore()
    for way in range(3):
        @pl.when(exists[way])
        def _():
            pl.semaphore_signal(barrier, inc=1, device_id={"row": targets[way]}, device_id_type=MESH)
    for bit in bits:
        pl.semaphore_signal(barrier, inc=1, device_id={"col": flip(bit)}, device_id_type=MESH)
    pl.semaphore_wait(
        barrier,
        1 + len(bits) + jnp.minimum(level, 1) + jnp.minimum(levels - 1 - level, 1),
    )

    @pl.when(mine > col)
    def _():
        send_own(0)

    @pl.when(mine <= col)
    def _():
        load_own(0).wait()

    def send_later():
        for q in range(1, rb):
            send_own(q)

    @pl.when(mine < 1)
    def _():
        send_later()

    @pl.loop(0, tiles)
    def _(t):
        load(0, t).wait()

    def produce(t, before):
        tile, h = t // fold, t % fold

        @pl.when(h == 0)
        def _():
            @pl.loop(0, inv_index - 1)
            def _(j):
                acc[0, tile] -= jnp.dot(
                    lower[0, j], natural[j, tile], preferred_element_type=jnp.float32
                )

        base = turn(acc[0, tile], -h * part)
        if before:
            prev = inv_index - 1
            base = base - jnp.dot(
                lower[0, prev], spread(low[prev, t]), preferred_element_type=jnp.float32
            )
        low[inv_index, t] = pack(
            jnp.dot(inv[...], base.astype(jnp.bfloat16), preferred_element_type=jnp.float32)
        )
        forward(inv_index, t)
        group = lax.broadcasted_iota(jnp.int32, (block, width), 1) // part
        acc[0, tile] = jnp.where(group == h, turn(base, h * part), acc[0, tile])

        @pl.when(h == fold - 1)
        def _():
            store_rem(0, tile).start()
            unpack(inv_index, tile)

    @pl.when(mine >= 0)
    def _():
        load_inv.wait()

    @pl.when(mine == 0)
    def _():
        @pl.loop(0, chunks)
        def _(t):
            produce(t, False)

    @pl.when(mine < 0)
    def _():
        @pl.loop(0, tiles)
        def _(t):
            store_rem(0, t).start()

    last = steps - 1 - side
    gather_at = last * chunks

    def update(tile, start, stop):
        for q in range(1, rb):
            @pl.loop(start, stop)
            def _(j):
                acc[q, tile] -= jnp.dot(
                    lower[q, j], natural[j, tile], preferred_element_type=jnp.float32
                )

    @pl.loop(0, steps * chunks)
    def _(e):
        inner = e % (2 * chunks)
        k_plain, t_plain = e // chunks, e % chunks
        k_pair, t_pair = 2 * (e // (2 * chunks)) + 1 - inner % 2, inner // 2
        k = k_plain + side * (k_pair - k_plain)
        t = t_plain + side * (t_pair - t_plain)

        @pl.when((e == chunks) & (mine >= 1))
        def _():
            send_later()

        @pl.when(e == gather_at)
        def _():
            for q in range(1, rb):
                @pl.loop(0, n_cols)
                def _(j):
                    receive_block(q, j)

                @pl.loop(0, tiles)
                def _(u):
                    load(q, u).wait()

            @pl.when(mine < 0)
            def _():
                @pl.loop(0, tiles)
                def _(u):
                    update(u, 0, last)

        @pl.when(mine != k)
        def _():
            send_low(0, k, t).wait_recv()
            forward(k, t)

            @pl.when(t % fold == fold - 1)
            def _():
                unpack(k, t // fold)

        @pl.when(mine == k + 1)
        def _():
            @pl.when(t == 0)
            def _():
                @pl.loop(0, inv_index)
                def _(j):
                    receive_block(0, j)

            produce(t, True)

        @pl.when((k == last) & (t % fold == fold - 1) & (mine < 0))
        def _():
            tile = t // fold
            update(tile, last, steps)
            for q in range(1, rb):
                store_rem(q, tile).start()

    @pl.when(mine >= 0)
    def _():
        @pl.loop(0, tiles)
        def _(u):
            update(u, 0, steps)
            for q in range(1, rb):
                store_rem(q, u).start()

    for k in range(steps):
        for way in range(3):
            @pl.when(goes(way, k))
            def _():
                pltpu.make_async_remote_copy(
                    src_ref=low.at[k], dst_ref=low.at[k],
                    send_sem=send_sem.at[way, k], recv_sem=recv_sem.at[k, 0],
                    device_id={"row": targets[way]}, device_id_type=MESH,
                ).wait_send()
    for q in range(rb):
        for j in range(n_cols):
            used = mine > j if q == 0 else mine >= -n_rows
            for b in range(len(bits)):
                @pl.when(used & passes(j, b))
                def _():
                    send_block(q, j, b).wait_send()
    for k in range(steps):
        pltpu.make_async_copy(natural.at[k], natural.at[k], low_sem.at[k]).wait()
    for q in range(rb):
        pltpu.make_async_copy(acc.at[q], acc.at[q], rem_sem.at[q]).wait()


def on_device(n_rows, n_cols, panel, rhs, inverse):
    rb, block = panel.shape[0], panel.shape[2]
    cols = rhs.shape[3]
    steps = inverse.shape[0]
    assert panel.shape[3] == 1 and n_cols == steps
    assert n_rows % 2 == 0 and steps % 2 == 0 and n_cols & (n_cols - 1) == 0
    width = 128 if cols % 128 == 0 else cols
    tiles = cols // width
    fold = 2
    bits = n_cols.bit_length() - 1
    dma = pltpu.SemaphoreType.DMA
    low, remainder = pl.pallas_call(
        functools.partial(kernel, n_rows, n_cols, steps),
        out_shape=(
            jax.ShapeDtypeStruct((steps, block, cols), jnp.bfloat16),
            jax.ShapeDtypeStruct((rb, block, cols), jnp.float32),
        ),
        in_specs=[pl.BlockSpec(memory_space=pltpu.HBM)] * 3,
        out_specs=(pl.BlockSpec(memory_space=pl.ANY),) * 2,
        scratch_shapes=[
            pltpu.VMEM((steps, tiles * fold, block // fold, width), jnp.bfloat16),
            pltpu.VMEM((steps, tiles, block, width), jnp.bfloat16),
            pltpu.VMEM((rb, tiles, block, width), jnp.float32),
            pltpu.VMEM((block, block), jnp.bfloat16),
            pltpu.VMEM((rb, steps, block, block), jnp.bfloat16),
            dma((rb, tiles)),
            dma((rb,)),
            dma,
            dma((steps,)),
            dma((rb,)),
            dma((3, steps)),
            dma((steps, tiles * fold)),
            dma((rb, n_cols, bits)),
            dma((rb, n_cols)),
        ],
        compiler_params=pltpu.CompilerParams(
            collective_id=0, has_side_effects=True, vmem_limit_bytes=40 * 2**20
        ),
    )(*(
        pltpu.with_memory_space_constraint(x, pltpu.HBM)
        for x in (panel.reshape(rb, block, block), rhs.reshape(rb, block, cols), inverse)
    ))
    return low.astype(jnp.float32), remainder.reshape(rhs.shape)


def solution(mesh):
    placed = (P(None, "row", None, "col", None), P(None, "row", None, "col"), P())
    return jax.shard_map(
        functools.partial(on_device, mesh.shape["row"], mesh.shape["col"]),
        mesh=mesh,
        in_specs=placed,
        out_specs=(P(None, None, "col"), P(None, "row", None, "col")),
        check_vma=False,
    )
```

```python
import functools

import jax
import jax.numpy as jnp
from jax import lax
from jax.experimental import pallas as pl
from jax.experimental.pallas import tpu as pltpu
from jax.sharding import PartitionSpec as P

MESH = pl.DeviceIdType.MESH


def kernel(
    n_rows, n_cols, steps, panel, rhs, inverse, low_out, rem_out,
    low, natural, acc, inv, lower,
    load_sem, own_sem, inv_sem, low_sem, rem_sem, send_sem, recv_sem, psend_sem, precv_sem,
):
    rb = acc.shape[0]
    tiles, block, width = acc.shape[1:]
    chunks = low.shape[1]
    fold = chunks // tiles
    part, height = width // fold, block // fold
    offset = n_rows - steps
    levels = n_rows // 2
    bits = [1 << b for b in reversed(range(n_cols.bit_length() - 1))]
    row, col = lax.axis_index("row"), lax.axis_index("col")
    level, side = row // 2, row % 2
    mine = row - offset
    inv_index = jnp.maximum(mine, 0)

    def flip(bit):
        return col + bit - 2 * bit * ((col // bit) % 2)

    targets = (row + 1 - 2 * side, row - 2, row + 2)
    exists = (level >= 0, level > 0, level < levels - 1)

    def columns(t):
        return pl.ds(pl.multiple_of(t * width, width), width)

    def load(q, t):
        return pltpu.make_async_copy(rhs.at[q, :, columns(t)], acc.at[q, t], load_sem.at[q, t])

    def load_own(q):
        return pltpu.make_async_copy(panel.at[q], lower.at[q, col], own_sem.at[q])

    load_inv = pltpu.make_async_copy(inverse.at[inv_index], inv, inv_sem)

    def store_low(k, t):
        return pltpu.make_async_copy(natural.at[k, t], low_out.at[k, :, columns(t)], low_sem.at[k])

    def store_rem(q, t):
        return pltpu.make_async_copy(acc.at[q, t], rem_out.at[q, :, columns(t)], rem_sem.at[q])

    def send_low(way, k, t):
        return pltpu.make_async_remote_copy(
            src_ref=low.at[k, t], dst_ref=low.at[k, t],
            send_sem=send_sem.at[way, k], recv_sem=recv_sem.at[k, t],
            device_id={"row": targets[way]}, device_id_type=MESH,
        )

    def goes(way, k):
        home = (offset + k) // 2
        same = k % 2 == side
        if way == 0:
            return same
        if way == 1:
            return same & (level > 0) & (level <= home)
        return same & (level < levels - 1) & (level >= home)

    def forward(k, t):
        for way in range(3):
            @pl.when(goes(way, k))
            def _():
                send_low(way, k, t).start()

    lane = lax.broadcasted_iota(jnp.int32, (height, width), 1) // part

    def turn(x, shift):
        return pltpu.roll(x, lax.rem(shift + width, width), 1)

    def spread(p):
        wide = p.astype(jnp.float32)
        return jnp.concatenate(
            [wide] + [pltpu.roll(wide, width - g * part, 1) for g in range(1, fold)], axis=0
        ).astype(jnp.bfloat16)

    def pack(x):
        out = x[:height]
        for g in range(1, fold):
            moved = pltpu.roll(x[g * height : (g + 1) * height], g * part, 1)
            out = jnp.where(lane == g, moved, out)
        return out.astype(jnp.bfloat16)

    def unpack(k, tile):
        held = [low[k, tile * fold + h].astype(jnp.float32) for h in range(fold)]
        for g in range(fold):
            out = held[0] if g == 0 else pltpu.roll(held[0], width - g * part, 1)
            for h in range(1, fold):
                shift = (h - g) * part % width
                moved = held[h] if shift == 0 else pltpu.roll(held[h], shift, 1)
                out = jnp.where(lane == h, moved, out)
            natural[k, tile, pl.ds(g * height, height), :] = out.astype(jnp.bfloat16)
        store_low(k, tile).start()

    def send_block(q, j, b):
        return pltpu.make_async_remote_copy(
            src_ref=lower.at[q, j], dst_ref=lower.at[q, j],
            send_sem=psend_sem.at[q, j, b], recv_sem=precv_sem.at[q, j],
            device_id={"col": flip(bits[b])}, device_id_type=MESH,
        )

    def send_own(q):
        load_own(q).wait()
        for b in range(len(bits)):
            send_block(q, col, b).start()

    def passes(j, b):
        return (col % (2 * bits[b])) == (j % (2 * bits[b]))

    def receive_block(q, j):
        @pl.when(col != j)
        def _():
            send_block(q, j, 0).wait_recv()
            for b in range(len(bits)):
                @pl.when(passes(j, b))
                def _():
                    send_block(q, j, b).start()

    @pl.when(mine >= 0)
    def _():
        load_inv.start()

    @pl.loop(0, tiles)
    def _(t):
        load(0, t).start()

    for q in range(rb):
        load_own(q).start()
    for q in range(1, rb):
        @pl.loop(0, tiles)
        def _(t):
            load(q, t).start()

    barrier = pltpu.get_barrier_semaphore()
    for way in range(3):
        @pl.when(exists[way])
        def _():
            pl.semaphore_signal(barrier, inc=1, device_id={"row": targets[way]}, device_id_type=MESH)
    for bit in bits:
        pl.semaphore_signal(barrier, inc=1, device_id={"col": flip(bit)}, device_id_type=MESH)
    pl.semaphore_wait(
        barrier,
        1 + len(bits) + jnp.minimum(level, 1) + jnp.minimum(levels - 1 - level, 1),
    )

    @pl.when(mine > col)
    def _():
        send_own(0)

    @pl.when(mine <= col)
    def _():
        load_own(0).wait()

    def send_later():
        for q in range(1, rb):
            send_own(q)

    @pl.when(mine < 0)
    def _():
        send_later()

    @pl.loop(0, tiles)
    def _(t):
        load(0, t).wait()

    def produce(t, before):
        tile, h = t // fold, t % fold

        @pl.when(h == 0)
        def _():
            @pl.loop(0, inv_index - 1)
            def _(j):
                acc[0, tile] -= jnp.dot(
                    lower[0, j], natural[j, tile], preferred_element_type=jnp.float32
                )

        base = turn(acc[0, tile], -h * part)
        if before:
            prev = inv_index - 1
            base = base - jnp.dot(
                lower[0, prev], spread(low[prev, t]), preferred_element_type=jnp.float32
            )
        low[inv_index, t] = pack(
            jnp.dot(inv[...], base.astype(jnp.bfloat16), preferred_element_type=jnp.float32)
        )
        forward(inv_index, t)
        group = lax.broadcasted_iota(jnp.int32, (block, width), 1) // part
        acc[0, tile] = jnp.where(group == h, turn(base, h * part), acc[0, tile])

        @pl.when(h == fold - 1)
        def _():
            store_rem(0, tile).start()
            unpack(inv_index, tile)

    @pl.when(mine >= 0)
    def _():
        load_inv.wait()

    @pl.when(mine == 0)
    def _():
        @pl.loop(0, chunks)
        def _(t):
            produce(t, False)

        send_later()

    @pl.when(mine < 0)
    def _():
        @pl.loop(0, tiles)
        def _(t):
            store_rem(0, t).start()

    last = steps - 1 - side
    gather_at = last * chunks

    def gather():
        for q in range(1, rb):
            @pl.loop(0, n_cols)
            def _(j):
                receive_block(q, j)

            @pl.loop(0, tiles)
            def _(u):
                load(q, u).wait()

    def update(tile, start, stop):
        for q in range(1, rb):
            @pl.loop(start, stop)
            def _(j):
                acc[q, tile] -= jnp.dot(
                    lower[q, j], natural[j, tile], preferred_element_type=jnp.float32
                )

    @pl.loop(0, steps * chunks)
    def _(e):
        inner = e % (2 * chunks)
        k_plain, t_plain = e // chunks, e % chunks
        k_pair, t_pair = 2 * (e // (2 * chunks)) + 1 - inner % 2, inner // 2
        k = k_plain + side * (k_pair - k_plain)
        t = t_plain + side * (t_pair - t_plain)

        @pl.when((e == (mine + side) * chunks) & (mine >= 1))
        def _():
            send_later()

        @pl.when((e == gather_at) & (mine < 0))
        def _():
            gather()

            @pl.loop(0, tiles)
            def _(u):
                update(u, 0, last)

        @pl.when(mine != k)
        def _():
            send_low(0, k, t).wait_recv()
            forward(k, t)

            @pl.when(t % fold == fold - 1)
            def _():
                unpack(k, t // fold)

        @pl.when(mine == k + 1)
        def _():
            @pl.when(t == 0)
            def _():
                @pl.loop(0, inv_index)
                def _(j):
                    receive_block(0, j)

            produce(t, True)

        @pl.when((k == last) & (t % fold == fold - 1) & (mine < 0))
        def _():
            tile = t // fold
            update(tile, last, steps)
            for q in range(1, rb):
                store_rem(q, tile).start()

    @pl.when(mine == steps - 1)
    def _():
        send_later()

    @pl.when(mine >= 0)
    def _():
        gather()

        @pl.loop(0, tiles)
        def _(u):
            update(u, 0, steps)
            for q in range(1, rb):
                store_rem(q, u).start()

    for k in range(steps):
        for way in range(3):
            @pl.when(goes(way, k))
            def _():
                pltpu.make_async_remote_copy(
                    src_ref=low.at[k], dst_ref=low.at[k],
                    send_sem=send_sem.at[way, k], recv_sem=recv_sem.at[k, 0],
                    device_id={"row": targets[way]}, device_id_type=MESH,
                ).wait_send()
    for q in range(rb):
        for j in range(n_cols):
            used = mine > j if q == 0 else mine >= -n_rows
            for b in range(len(bits)):
                @pl.when(used & passes(j, b))
                def _():
                    send_block(q, j, b).wait_send()
    for k in range(steps):
        pltpu.make_async_copy(natural.at[k], natural.at[k], low_sem.at[k]).wait()
    for q in range(rb):
        pltpu.make_async_copy(acc.at[q], acc.at[q], rem_sem.at[q]).wait()


def on_device(n_rows, n_cols, panel, rhs, inverse):
    rb, block = panel.shape[0], panel.shape[2]
    cols = rhs.shape[3]
    steps = inverse.shape[0]
    assert panel.shape[3] == 1 and n_cols == steps
    assert n_rows % 2 == 0 and steps % 2 == 0 and n_cols & (n_cols - 1) == 0
    width = 128 if cols % 128 == 0 else cols
    tiles = cols // width
    fold = 2
    bits = n_cols.bit_length() - 1
    dma = pltpu.SemaphoreType.DMA
    low, remainder = pl.pallas_call(
        functools.partial(kernel, n_rows, n_cols, steps),
        out_shape=(
            jax.ShapeDtypeStruct((steps, block, cols), jnp.bfloat16),
            jax.ShapeDtypeStruct((rb, block, cols), jnp.float32),
        ),
        in_specs=[pl.BlockSpec(memory_space=pltpu.HBM)] * 3,
        out_specs=(pl.BlockSpec(memory_space=pl.ANY),) * 2,
        scratch_shapes=[
            pltpu.VMEM((steps, tiles * fold, block // fold, width), jnp.bfloat16),
            pltpu.VMEM((steps, tiles, block, width), jnp.bfloat16),
            pltpu.VMEM((rb, tiles, block, width), jnp.float32),
            pltpu.VMEM((block, block), jnp.bfloat16),
            pltpu.VMEM((rb, steps, block, block), jnp.bfloat16),
            dma((rb, tiles)),
            dma((rb,)),
            dma,
            dma((steps,)),
            dma((rb,)),
            dma((3, steps)),
            dma((steps, tiles * fold)),
            dma((rb, n_cols, bits)),
            dma((rb, n_cols)),
        ],
        compiler_params=pltpu.CompilerParams(
            collective_id=0, has_side_effects=True, vmem_limit_bytes=40 * 2**20
        ),
    )(*(
        pltpu.with_memory_space_constraint(x, pltpu.HBM)
        for x in (panel.reshape(rb, block, block), rhs.reshape(rb, block, cols), inverse)
    ))
    return low.astype(jnp.float32), remainder.reshape(rhs.shape)


def solution(mesh):
    placed = (P(None, "row", None, "col", None), P(None, "row", None, "col"), P())
    return jax.shard_map(
        functools.partial(on_device, mesh.shape["row"], mesh.shape["col"]),
        mesh=mesh,
        in_specs=placed,
        out_specs=(P(None, None, "col"), P(None, "row", None, "col")),
        check_vma=False,
    )
```

```python
import functools

import jax
import jax.numpy as jnp
from jax import lax
from jax.experimental import pallas as pl
from jax.experimental.pallas import tpu as pltpu
from jax.sharding import PartitionSpec as P

MESH = pl.DeviceIdType.MESH


def kernel(
    n_rows, n_cols, steps, panel, rhs, inverse, low_out, rem_out,
    low, natural, acc, inv, lower,
    load_sem, own_sem, inv_sem, low_sem, rem_sem, send_sem, recv_sem, psend_sem, precv_sem,
):
    rb = acc.shape[0]
    tiles, block, width = acc.shape[1:]
    chunks = low.shape[1]
    fold = chunks // tiles
    part, height = width // fold, block // fold
    offset = n_rows - steps
    levels = n_rows // 2
    bits = [1 << b for b in reversed(range(n_cols.bit_length() - 1))]
    row, col = lax.axis_index("row"), lax.axis_index("col")
    level, side = row // 2, row % 2
    mine = row - offset
    inv_index = jnp.maximum(mine, 0)

    def flip(bit):
        return col + bit - 2 * bit * ((col // bit) % 2)

    targets = (row + 1 - 2 * side, row - 2, row + 2)
    exists = (level >= 0, level > 0, level < levels - 1)

    def columns(t):
        return pl.ds(pl.multiple_of(t * width, width), width)

    def load(q, t):
        return pltpu.make_async_copy(rhs.at[q, :, columns(t)], acc.at[q, t], load_sem.at[q, t])

    def load_own(q):
        return pltpu.make_async_copy(panel.at[q], lower.at[q, col], own_sem.at[q])

    load_inv = pltpu.make_async_copy(inverse.at[inv_index], inv, inv_sem)

    def store_low(k, t):
        return pltpu.make_async_copy(natural.at[k, t], low_out.at[k, :, columns(t)], low_sem.at[k])

    def store_rem(q, t):
        return pltpu.make_async_copy(acc.at[q, t], rem_out.at[q, :, columns(t)], rem_sem.at[q])

    def send_low(way, k, t):
        return pltpu.make_async_remote_copy(
            src_ref=low.at[k, t], dst_ref=low.at[k, t],
            send_sem=send_sem.at[way, k], recv_sem=recv_sem.at[k, t],
            device_id={"row": targets[way]}, device_id_type=MESH,
        )

    def goes(way, k):
        home = (offset + k) // 2
        same = k % 2 == side
        if way == 0:
            return same
        if way == 1:
            return same & (level > 0) & (level <= home)
        return same & (level < levels - 1) & (level >= home)

    def forward(k, t):
        for way, when in ((0, side == 0), (2, True), (1, True), (0, side == 1)):
            @pl.when(goes(way, k) & when)
            def _():
                send_low(way, k, t).start()

    lane = lax.broadcasted_iota(jnp.int32, (height, width), 1) // part

    def turn(x, shift):
        return pltpu.roll(x, lax.rem(shift + width, width), 1)

    def spread(p):
        wide = p.astype(jnp.float32)
        return jnp.concatenate(
            [wide] + [pltpu.roll(wide, width - g * part, 1) for g in range(1, fold)], axis=0
        ).astype(jnp.bfloat16)

    def pack(x):
        out = x[:height]
        for g in range(1, fold):
            moved = pltpu.roll(x[g * height : (g + 1) * height], g * part, 1)
            out = jnp.where(lane == g, moved, out)
        return out.astype(jnp.bfloat16)

    def unpack(k, tile):
        held = [low[k, tile * fold + h].astype(jnp.float32) for h in range(fold)]
        for g in range(fold):
            out = held[0] if g == 0 else pltpu.roll(held[0], width - g * part, 1)
            for h in range(1, fold):
                shift = (h - g) * part % width
                moved = held[h] if shift == 0 else pltpu.roll(held[h], shift, 1)
                out = jnp.where(lane == h, moved, out)
            natural[k, tile, pl.ds(g * height, height), :] = out.astype(jnp.bfloat16)
        store_low(k, tile).start()

    def send_block(q, j, b):
        return pltpu.make_async_remote_copy(
            src_ref=lower.at[q, j], dst_ref=lower.at[q, j],
            send_sem=psend_sem.at[q, j, b], recv_sem=precv_sem.at[q, j],
            device_id={"col": flip(bits[b])}, device_id_type=MESH,
        )

    def send_own(q):
        load_own(q).wait()
        for b in reversed(range(len(bits))):
            send_block(q, col, b).start()

    def send_piece(p):
        rows = pl.ds(pl.multiple_of(p * (block // chunks), block // chunks), block // chunks)
        for q in range(1, rb):
            @pl.when(p == 0)
            def _():
                load_own(q).wait()

            for b in reversed(range(len(bits))):
                pltpu.make_async_remote_copy(
                    src_ref=lower.at[q, col, rows], dst_ref=lower.at[q, col, rows],
                    send_sem=psend_sem.at[q, col, b], recv_sem=precv_sem.at[q, col],
                    device_id={"col": flip(bits[b])}, device_id_type=MESH,
                ).start()

    def passes(j, b):
        return (col % (2 * bits[b])) == (j % (2 * bits[b]))

    def receive_block(q, j):
        @pl.when(col != j)
        def _():
            send_block(q, j, 0).wait_recv()
            for b in reversed(range(len(bits))):
                @pl.when(passes(j, b))
                def _():
                    send_block(q, j, b).start()

    @pl.when(mine >= 0)
    def _():
        load_inv.start()

    @pl.loop(0, tiles)
    def _(t):
        load(0, t).start()

    for q in range(rb):
        load_own(q).start()
    for q in range(1, rb):
        @pl.loop(0, tiles)
        def _(t):
            load(q, t).start()

    barrier = pltpu.get_barrier_semaphore()
    for way in range(3):
        @pl.when(exists[way])
        def _():
            pl.semaphore_signal(barrier, inc=1, device_id={"row": targets[way]}, device_id_type=MESH)
    for bit in bits:
        pl.semaphore_signal(barrier, inc=1, device_id={"col": flip(bit)}, device_id_type=MESH)
    pl.semaphore_wait(
        barrier,
        1 + len(bits) + jnp.minimum(level, 1) + jnp.minimum(levels - 1 - level, 1),
    )

    @pl.when(mine > col)
    def _():
        send_own(0)

    @pl.when(mine <= col)
    def _():
        load_own(0).wait()

    def send_later():
        for q in range(1, rb):
            send_own(q)

    @pl.when(mine < 0)
    def _():
        send_later()

    @pl.loop(0, tiles)
    def _(t):
        load(0, t).wait()

    def produce(t, before):
        tile, h = t // fold, t % fold

        @pl.when(h == 0)
        def _():
            @pl.loop(0, inv_index - 1)
            def _(j):
                acc[0, tile] -= jnp.dot(
                    lower[0, j], natural[j, tile], preferred_element_type=jnp.float32
                )

        base = turn(acc[0, tile], -h * part)
        if before:
            prev = inv_index - 1
            base = base - jnp.dot(
                lower[0, prev], spread(low[prev, t]), preferred_element_type=jnp.float32
            )
        low[inv_index, t] = pack(
            jnp.dot(inv[...], base.astype(jnp.bfloat16), preferred_element_type=jnp.float32)
        )
        forward(inv_index, t)
        group = lax.broadcasted_iota(jnp.int32, (block, width), 1) // part
        acc[0, tile] = jnp.where(group == h, turn(base, h * part), acc[0, tile])

        @pl.when(h == fold - 1)
        def _():
            store_rem(0, tile).start()
            unpack(inv_index, tile)

    @pl.when(mine >= 0)
    def _():
        load_inv.wait()

    @pl.when(mine == 0)
    def _():
        @pl.loop(0, chunks)
        def _(t):
            produce(t, False)

        send_later()

    @pl.when(mine < 0)
    def _():
        @pl.loop(0, tiles)
        def _(t):
            store_rem(0, t).start()

    last = steps - 1 - side
    gather_at = last * chunks

    def gather():
        for q in range(1, rb):
            @pl.loop(0, n_cols)
            def _(j):
                receive_block(q, j)

            @pl.loop(0, tiles)
            def _(u):
                load(q, u).wait()

    def update(tile, start, stop):
        for q in range(1, rb):
            @pl.loop(start, stop)
            def _(j):
                acc[q, tile] -= jnp.dot(
                    lower[q, j], natural[j, tile], preferred_element_type=jnp.float32
                )

    @pl.loop(0, steps * chunks)
    def _(e):
        inner = e % (2 * chunks)
        k_plain, t_plain = e // chunks, e % chunks
        k_pair, t_pair = 2 * (e // (2 * chunks)) + 1 - inner % 2, inner // 2
        k = k_plain + side * (k_pair - k_plain)
        t = t_plain + side * (t_pair - t_plain)

        @pl.when((e == mine * chunks) & (mine >= 1) & (side == 0))
        def _():
            send_later()

        begin = (mine + 1) * chunks

        @pl.when((mine >= 1) & (side == 1) & (e == begin))
        def _():
            @pl.loop(0, chunks // 2)
            def _(p):
                send_piece(p)

        @pl.when((mine >= 1) & (side == 1) & (e > begin) & (e <= begin + chunks // 2))
        def _():
            send_piece(e - begin - 1 + chunks // 2)

        @pl.when((e == gather_at) & ((mine < 0) | (side == 0)))
        def _():
            gather()

            @pl.loop(0, tiles)
            def _(u):
                update(u, 0, last)

        @pl.when(mine != k)
        def _():
            send_low(0, k, t).wait_recv()
            forward(k, t)

            @pl.when(t % fold == fold - 1)
            def _():
                unpack(k, t // fold)

        @pl.when(mine == k + 1)
        def _():
            @pl.when(t == 0)
            def _():
                @pl.loop(0, inv_index)
                def _(j):
                    receive_block(0, j)

            produce(t, True)

            @pl.when(mine == steps - 1)
            def _():
                send_piece(t)

        @pl.when((k == last) & (t % fold == fold - 1) & ((mine < 0) | (side == 0)))
        def _():
            tile = t // fold
            update(tile, last, steps)
            for q in range(1, rb):
                store_rem(q, tile).start()

    @pl.when((mine >= 0) & (side == 1))
    def _():
        gather()

        @pl.loop(0, tiles)
        def _(u):
            update(u, 0, steps)
            for q in range(1, rb):
                store_rem(q, u).start()

    for k in range(steps):
        for way in range(3):
            @pl.when(goes(way, k))
            def _():
                pltpu.make_async_remote_copy(
                    src_ref=low.at[k], dst_ref=low.at[k],
                    send_sem=send_sem.at[way, k], recv_sem=recv_sem.at[k, 0],
                    device_id={"row": targets[way]}, device_id_type=MESH,
                ).wait_send()
    for q in range(rb):
        for j in range(n_cols):
            used = mine > j if q == 0 else mine >= -n_rows
            for b in range(len(bits)):
                @pl.when(used & passes(j, b))
                def _():
                    send_block(q, j, b).wait_send()
    for k in range(steps):
        pltpu.make_async_copy(natural.at[k], natural.at[k], low_sem.at[k]).wait()
    for q in range(rb):
        pltpu.make_async_copy(acc.at[q], acc.at[q], rem_sem.at[q]).wait()


def on_device(n_rows, n_cols, panel, rhs, inverse):
    rb, block = panel.shape[0], panel.shape[2]
    cols = rhs.shape[3]
    steps = inverse.shape[0]
    assert panel.shape[3] == 1 and n_cols == steps
    assert n_rows % 2 == 0 and steps % 2 == 0 and n_cols & (n_cols - 1) == 0
    width = 128 if cols % 128 == 0 else cols
    tiles = cols // width
    fold = 2
    bits = n_cols.bit_length() - 1
    dma = pltpu.SemaphoreType.DMA
    low, remainder = pl.pallas_call(
        functools.partial(kernel, n_rows, n_cols, steps),
        out_shape=(
            jax.ShapeDtypeStruct((steps, block, cols), jnp.bfloat16),
            jax.ShapeDtypeStruct((rb, block, cols), jnp.float32),
        ),
        in_specs=[pl.BlockSpec(memory_space=pltpu.HBM)] * 3,
        out_specs=(pl.BlockSpec(memory_space=pl.ANY),) * 2,
        scratch_shapes=[
            pltpu.VMEM((steps, tiles * fold, block // fold, width), jnp.bfloat16),
            pltpu.VMEM((steps, tiles, block, width), jnp.bfloat16),
            pltpu.VMEM((rb, tiles, block, width), jnp.float32),
            pltpu.VMEM((block, block), jnp.bfloat16),
            pltpu.VMEM((rb, steps, block, block), jnp.bfloat16),
            dma((rb, tiles)),
            dma((rb,)),
            dma,
            dma((steps,)),
            dma((rb,)),
            dma((3, steps)),
            dma((steps, tiles * fold)),
            dma((rb, n_cols, bits)),
            dma((rb, n_cols)),
        ],
        compiler_params=pltpu.CompilerParams(
            collective_id=0, has_side_effects=True, vmem_limit_bytes=40 * 2**20
        ),
    )(*(
        pltpu.with_memory_space_constraint(x, pltpu.HBM)
        for x in (panel.reshape(rb, block, block), rhs.reshape(rb, block, cols), inverse)
    ))
    return low.astype(jnp.float32), remainder.reshape(rhs.shape)


def solution(mesh):
    placed = (P(None, "row", None, "col", None), P(None, "row", None, "col"), P())
    return jax.shard_map(
        functools.partial(on_device, mesh.shape["row"], mesh.shape["col"]),
        mesh=mesh,
        in_specs=placed,
        out_specs=(P(None, None, "col"), P(None, "row", None, "col")),
        check_vma=False,
    )
```

```python
import functools

import jax
import jax.numpy as jnp
from jax import lax
from jax.experimental import pallas as pl
from jax.experimental.pallas import tpu as pltpu
from jax.sharding import PartitionSpec as P

MESH = pl.DeviceIdType.MESH


def kernel(
    n_rows, n_cols, steps, panel, rhs, inverse, low_out, rem_out,
    low, natural, acc, inv, lower,
    load_sem, own_sem, inv_sem, low_sem, rem_sem, send_sem, recv_sem, psend_sem, precv_sem,
):
    rb = acc.shape[0]
    tiles, block, width = acc.shape[1:]
    chunks = low.shape[1]
    fold = chunks // tiles
    part, height = width // fold, block // fold
    offset = n_rows - steps
    levels = n_rows // 2
    bits = [1 << b for b in reversed(range(n_cols.bit_length() - 1))]
    row, col = lax.axis_index("row"), lax.axis_index("col")
    level, side = row // 2, row % 2
    mine = row - offset
    inv_index = jnp.maximum(mine, 0)

    def flip(bit):
        return col + bit - 2 * bit * ((col // bit) % 2)

    targets = (row + 1 - 2 * side, row - 2, row + 2)
    exists = (level >= 0, level > 0, level < levels - 1)

    def columns(t):
        return pl.ds(pl.multiple_of(t * width, width), width)

    def load(q, t):
        return pltpu.make_async_copy(rhs.at[q, :, columns(t)], acc.at[q, t], load_sem.at[q, t])

    def load_own(q):
        return pltpu.make_async_copy(panel.at[q], lower.at[q, col], own_sem.at[q])

    load_inv = pltpu.make_async_copy(inverse.at[inv_index], inv, inv_sem)

    def store_low(k, t):
        return pltpu.make_async_copy(natural.at[k, t], low_out.at[k, :, columns(t)], low_sem.at[k])

    def store_rem(q, t):
        return pltpu.make_async_copy(acc.at[q, t], rem_out.at[q, :, columns(t)], rem_sem.at[q])

    def send_low(way, k, t):
        return pltpu.make_async_remote_copy(
            src_ref=low.at[k, t], dst_ref=low.at[k, t],
            send_sem=send_sem.at[way, k], recv_sem=recv_sem.at[k, t],
            device_id={"row": targets[way]}, device_id_type=MESH,
        )

    def goes(way, k):
        home = (offset + k) // 2
        same = k % 2 == side
        if way == 0:
            return same
        if way == 1:
            return same & (level > 0) & (level <= home)
        return same & (level < levels - 1) & (level >= home)

    def forward(k, t):
        for way, when in ((0, side == 0), (2, True), (1, True), (0, side == 1)):
            @pl.when(goes(way, k) & when)
            def _():
                send_low(way, k, t).start()

    lane = lax.broadcasted_iota(jnp.int32, (height, width), 1) // part

    def turn(x, shift):
        return pltpu.roll(x, lax.rem(shift + width, width), 1)

    def spread(p):
        wide = p.astype(jnp.float32)
        return jnp.concatenate(
            [wide] + [pltpu.roll(wide, width - g * part, 1) for g in range(1, fold)], axis=0
        ).astype(jnp.bfloat16)

    def pack(x):
        out = x[:height]
        for g in range(1, fold):
            moved = pltpu.roll(x[g * height : (g + 1) * height], g * part, 1)
            out = jnp.where(lane == g, moved, out)
        return out.astype(jnp.bfloat16)

    def unpack(k, tile):
        held = [low[k, tile * fold + h].astype(jnp.float32) for h in range(fold)]
        for g in range(fold):
            out = held[0] if g == 0 else pltpu.roll(held[0], width - g * part, 1)
            for h in range(1, fold):
                shift = (h - g) * part % width
                moved = held[h] if shift == 0 else pltpu.roll(held[h], shift, 1)
                out = jnp.where(lane == h, moved, out)
            natural[k, tile, pl.ds(g * height, height), :] = out.astype(jnp.bfloat16)
        store_low(k, tile).start()

    def send_block(q, j, b):
        return pltpu.make_async_remote_copy(
            src_ref=lower.at[q, j], dst_ref=lower.at[q, j],
            send_sem=psend_sem.at[q, j, b], recv_sem=precv_sem.at[q, j],
            device_id={"col": flip(bits[b])}, device_id_type=MESH,
        )

    def send_own(q):
        load_own(q).wait()
        for b in reversed(range(len(bits))):
            send_block(q, col, b).start()

    def send_piece(p):
        rows = pl.ds(pl.multiple_of(p * (block // chunks), block // chunks), block // chunks)
        for q in range(1, rb):
            @pl.when(p == 0)
            def _():
                load_own(q).wait()

            for b in reversed(range(len(bits))):
                pltpu.make_async_remote_copy(
                    src_ref=lower.at[q, col, rows], dst_ref=lower.at[q, col, rows],
                    send_sem=psend_sem.at[q, col, b], recv_sem=precv_sem.at[q, col],
                    device_id={"col": flip(bits[b])}, device_id_type=MESH,
                ).start()

    def passes(j, b):
        return (col % (2 * bits[b])) == (j % (2 * bits[b]))

    def receive_blocks(q, count):
        def duty(j):
            return (col != j) & passes(j, len(bits) - 1)

        @pl.loop(0, count)
        def _(j):
            @pl.when(duty(j))
            def _():
                send_block(q, j, 0).wait_recv()
                for b in reversed(range(len(bits))):
                    @pl.when(passes(j, b))
                    def _():
                        send_block(q, j, b).start()

        @pl.loop(0, count)
        def _(j):
            @pl.when((col != j) & jnp.logical_not(duty(j)))
            def _():
                send_block(q, j, 0).wait_recv()

    @pl.when(mine >= 0)
    def _():
        load_inv.start()

    @pl.loop(0, tiles)
    def _(t):
        load(0, t).start()

    for q in range(rb):
        load_own(q).start()
    for q in range(1, rb):
        @pl.loop(0, tiles)
        def _(t):
            load(q, t).start()

    barrier = pltpu.get_barrier_semaphore()
    for way in range(3):
        @pl.when(exists[way])
        def _():
            pl.semaphore_signal(barrier, inc=1, device_id={"row": targets[way]}, device_id_type=MESH)
    for bit in bits:
        pl.semaphore_signal(barrier, inc=1, device_id={"col": flip(bit)}, device_id_type=MESH)
    pl.semaphore_wait(
        barrier,
        1 + len(bits) + jnp.minimum(level, 1) + jnp.minimum(levels - 1 - level, 1),
    )

    @pl.when(mine > col)
    def _():
        send_own(0)

    @pl.when(mine <= col)
    def _():
        load_own(0).wait()

    def send_later():
        for q in range(1, rb):
            send_own(q)

    @pl.when(mine < 0)
    def _():
        send_later()

    @pl.loop(0, tiles)
    def _(t):
        load(0, t).wait()

    def produce(t, before):
        tile, h = t // fold, t % fold

        @pl.when((h == 0) & (side == 0))
        def _():
            @pl.loop(0, inv_index - 1)
            def _(j):
                acc[0, tile] -= jnp.dot(
                    lower[0, j], natural[j, tile], preferred_element_type=jnp.float32
                )

        base = turn(acc[0, tile], -h * part)
        if before:
            prev = inv_index - 1
            base = base - jnp.dot(
                lower[0, prev], spread(low[prev, t]), preferred_element_type=jnp.float32
            )
        low[inv_index, t] = pack(
            jnp.dot(inv[...], base.astype(jnp.bfloat16), preferred_element_type=jnp.float32)
        )
        forward(inv_index, t)
        group = lax.broadcasted_iota(jnp.int32, (block, width), 1) // part
        acc[0, tile] = jnp.where(group == h, turn(base, h * part), acc[0, tile])

        @pl.when(h == fold - 1)
        def _():
            store_rem(0, tile).start()
            unpack(inv_index, tile)

    @pl.when(mine >= 0)
    def _():
        load_inv.wait()

    @pl.when(mine == 0)
    def _():
        @pl.loop(0, chunks)
        def _(t):
            produce(t, False)

        send_later()

    @pl.when(mine < 0)
    def _():
        @pl.loop(0, tiles)
        def _(t):
            store_rem(0, t).start()

    last = steps - 1 - side
    gather_at = last * chunks

    def gather():
        for q in range(1, rb):
            receive_blocks(q, n_cols)

            @pl.loop(0, tiles)
            def _(u):
                load(q, u).wait()

    def update(tile, start, stop):
        for q in range(1, rb):
            @pl.loop(start, stop)
            def _(j):
                acc[q, tile] -= jnp.dot(
                    lower[q, j], natural[j, tile], preferred_element_type=jnp.float32
                )

    @pl.loop(0, steps * chunks)
    def _(e):
        inner = e % (2 * chunks)
        k_plain, t_plain = e // chunks, e % chunks
        k_pair, t_pair = 2 * (e // (2 * chunks)) + 1 - inner % 2, inner // 2
        k = k_plain + side * (k_pair - k_plain)
        t = t_plain + side * (t_pair - t_plain)

        @pl.when((e == mine * chunks) & (mine >= 1) & (side == 0))
        def _():
            send_later()

        begin = (mine + 1) * chunks

        @pl.when((mine >= 1) & (side == 1) & (e == begin))
        def _():
            @pl.loop(0, chunks // 2)
            def _(p):
                send_piece(p)

        @pl.when((mine >= 1) & (side == 1) & (e > begin) & (e <= begin + chunks // 2))
        def _():
            send_piece(e - begin - 1 + chunks // 2)

        @pl.when((e == gather_at) & ((mine < 0) | (side == 0)))
        def _():
            gather()

            @pl.loop(0, tiles)
            def _(u):
                update(u, 0, last)

        @pl.when(mine != k)
        def _():
            send_low(0, k, t).wait_recv()
            forward(k, t)

            @pl.when(t % fold == fold - 1)
            def _():
                unpack(k, t // fold)

        @pl.when((side == 1) & (k % 2 == 0) & (k + 3 <= mine) & (t % fold == fold - 1))
        def _():
            @pl.when((k == 0) & (t == fold - 1))
            def _():
                receive_blocks(0, inv_index)

            @pl.loop(k, k + 2)
            def _(j):
                acc[0, t // fold] -= jnp.dot(
                    lower[0, j], natural[j, t // fold], preferred_element_type=jnp.float32
                )

        @pl.when(mine == k + 1)
        def _():
            @pl.when((t == 0) & ((side == 0) | (mine == 1)))
            def _():
                receive_blocks(0, inv_index)

            produce(t, True)

            @pl.when(mine == steps - 1)
            def _():
                send_piece(t)

        @pl.when((k == last) & (t % fold == fold - 1) & ((mine < 0) | (side == 0)))
        def _():
            tile = t // fold
            update(tile, last, steps)
            for q in range(1, rb):
                store_rem(q, tile).start()

    @pl.when((mine >= 0) & (side == 1))
    def _():
        gather()

        @pl.loop(0, tiles)
        def _(u):
            update(u, 0, steps)
            for q in range(1, rb):
                store_rem(q, u).start()

    for k in range(steps):
        for way in range(3):
            @pl.when(goes(way, k))
            def _():
                pltpu.make_async_remote_copy(
                    src_ref=low.at[k], dst_ref=low.at[k],
                    send_sem=send_sem.at[way, k], recv_sem=recv_sem.at[k, 0],
                    device_id={"row": targets[way]}, device_id_type=MESH,
                ).wait_send()
    for q in range(rb):
        for j in range(n_cols):
            used = mine > j if q == 0 else mine >= -n_rows
            for b in range(len(bits)):
                @pl.when(used & passes(j, b))
                def _():
                    send_block(q, j, b).wait_send()
    for k in range(steps):
        pltpu.make_async_copy(natural.at[k], natural.at[k], low_sem.at[k]).wait()
    for q in range(rb):
        pltpu.make_async_copy(acc.at[q], acc.at[q], rem_sem.at[q]).wait()


def on_device(n_rows, n_cols, panel, rhs, inverse):
    rb, block = panel.shape[0], panel.shape[2]
    cols = rhs.shape[3]
    steps = inverse.shape[0]
    assert panel.shape[3] == 1 and n_cols == steps
    assert n_rows % 2 == 0 and steps % 2 == 0 and n_cols & (n_cols - 1) == 0
    width = 128 if cols % 128 == 0 else cols
    tiles = cols // width
    fold = 2
    bits = n_cols.bit_length() - 1
    dma = pltpu.SemaphoreType.DMA
    low, remainder = pl.pallas_call(
        functools.partial(kernel, n_rows, n_cols, steps),
        out_shape=(
            jax.ShapeDtypeStruct((steps, block, cols), jnp.bfloat16),
            jax.ShapeDtypeStruct((rb, block, cols), jnp.float32),
        ),
        in_specs=[pl.BlockSpec(memory_space=pltpu.HBM)] * 3,
        out_specs=(pl.BlockSpec(memory_space=pl.ANY),) * 2,
        scratch_shapes=[
            pltpu.VMEM((steps, tiles * fold, block // fold, width), jnp.bfloat16),
            pltpu.VMEM((steps, tiles, block, width), jnp.bfloat16),
            pltpu.VMEM((rb, tiles, block, width), jnp.float32),
            pltpu.VMEM((block, block), jnp.bfloat16),
            pltpu.VMEM((rb, steps, block, block), jnp.bfloat16),
            dma((rb, tiles)),
            dma((rb,)),
            dma,
            dma((steps,)),
            dma((rb,)),
            dma((3, steps)),
            dma((steps, tiles * fold)),
            dma((rb, n_cols, bits)),
            dma((rb, n_cols)),
        ],
        compiler_params=pltpu.CompilerParams(
            collective_id=0, has_side_effects=True, vmem_limit_bytes=40 * 2**20
        ),
    )(*(
        pltpu.with_memory_space_constraint(x, pltpu.HBM)
        for x in (panel.reshape(rb, block, block), rhs.reshape(rb, block, cols), inverse)
    ))
    return low.astype(jnp.float32), remainder.reshape(rhs.shape)


def solution(mesh):
    placed = (P(None, "row", None, "col", None), P(None, "row", None, "col"), P())
    return jax.shard_map(
        functools.partial(on_device, mesh.shape["row"], mesh.shape["col"]),
        mesh=mesh,
        in_specs=placed,
        out_specs=(P(None, None, "col"), P(None, "row", None, "col")),
        check_vma=False,
    )
```

```python
import functools

import jax
import jax.numpy as jnp
from jax import lax
from jax.experimental import pallas as pl
from jax.experimental.pallas import tpu as pltpu
from jax.sharding import PartitionSpec as P

MESH = pl.DeviceIdType.MESH


def kernel(
    n_rows, n_cols, steps, panel, rhs, inverse, low_out, rem_out,
    low, natural, acc, inv, lower,
    load_sem, own_sem, inv_sem, low_sem, rem_sem, send_sem, recv_sem, psend_sem, precv_sem,
):
    rb = acc.shape[0]
    tiles, block, width = acc.shape[1:]
    chunks = low.shape[1]
    fold = chunks // tiles
    part, height = width // fold, block // fold
    offset = n_rows - steps
    levels = n_rows // 2
    bits = [1 << b for b in reversed(range(n_cols.bit_length() - 1))]
    row, col = lax.axis_index("row"), lax.axis_index("col")
    level, side = row // 2, row % 2
    mine = row - offset
    inv_index = jnp.maximum(mine, 0)

    def flip(bit):
        return col + bit - 2 * bit * ((col // bit) % 2)

    targets = (row + 1 - 2 * side, row - 2, row + 2)
    exists = (level >= 0, level > 0, level < levels - 1)

    def columns(t):
        return pl.ds(pl.multiple_of(t * width, width), width)

    def load(q, t):
        return pltpu.make_async_copy(rhs.at[q, :, columns(t)], acc.at[q, t], load_sem.at[q, t])

    def load_own(q):
        return pltpu.make_async_copy(panel.at[q], lower.at[q, col], own_sem.at[q])

    load_inv = pltpu.make_async_copy(inverse.at[inv_index], inv, inv_sem)

    def store_low(k, t):
        return pltpu.make_async_copy(natural.at[k, t], low_out.at[k, :, columns(t)], low_sem.at[k])

    def store_rem(q, t):
        return pltpu.make_async_copy(acc.at[q, t], rem_out.at[q, :, columns(t)], rem_sem.at[q])

    def send_low(way, k, t):
        return pltpu.make_async_remote_copy(
            src_ref=low.at[k, t], dst_ref=low.at[k, t],
            send_sem=send_sem.at[way, k], recv_sem=recv_sem.at[k, t],
            device_id={"row": targets[way]}, device_id_type=MESH,
        )

    def goes(way, k):
        home = (offset + k) // 2
        same = k % 2 == side
        if way == 0:
            return same
        if way == 1:
            return same & (level > 0) & (level <= home)
        return same & (level < levels - 1) & (level >= home)

    def forward(k, t):
        for way, when in ((0, side == 0), (2, True), (1, True), (0, side == 1)):
            @pl.when(goes(way, k) & when)
            def _():
                send_low(way, k, t).start()

    lane = lax.broadcasted_iota(jnp.int32, (height, width), 1) // part

    def turn(x, shift):
        return pltpu.roll(x, lax.rem(shift + width, width), 1)

    def spread(p):
        wide = p.astype(jnp.float32)
        return jnp.concatenate(
            [wide] + [pltpu.roll(wide, width - g * part, 1) for g in range(1, fold)], axis=0
        ).astype(jnp.bfloat16)

    def pack(x):
        out = x[:height]
        for g in range(1, fold):
            moved = pltpu.roll(x[g * height : (g + 1) * height], g * part, 1)
            out = jnp.where(lane == g, moved, out)
        return out.astype(jnp.bfloat16)

    def unpack(k, tile):
        held = [low[k, tile * fold + h].astype(jnp.float32) for h in range(fold)]
        for g in range(fold):
            out = held[0] if g == 0 else pltpu.roll(held[0], width - g * part, 1)
            for h in range(1, fold):
                shift = (h - g) * part % width
                moved = held[h] if shift == 0 else pltpu.roll(held[h], shift, 1)
                out = jnp.where(lane == h, moved, out)
            natural[k, tile, pl.ds(g * height, height), :] = out.astype(jnp.bfloat16)
        store_low(k, tile).start()

    def send_block(q, j, b):
        return pltpu.make_async_remote_copy(
            src_ref=lower.at[q, j], dst_ref=lower.at[q, j],
            send_sem=psend_sem.at[q, j, b], recv_sem=precv_sem.at[q, j],
            device_id={"col": flip(bits[b])}, device_id_type=MESH,
        )

    def send_own(q):
        load_own(q).wait()
        for b in reversed(range(len(bits))):
            send_block(q, col, b).start()

    def send_piece(p):
        rows = pl.ds(pl.multiple_of(p * (block // chunks), block // chunks), block // chunks)
        for q in range(1, rb):
            @pl.when(p == 0)
            def _():
                load_own(q).wait()

            for b in reversed(range(len(bits))):
                pltpu.make_async_remote_copy(
                    src_ref=lower.at[q, col, rows], dst_ref=lower.at[q, col, rows],
                    send_sem=psend_sem.at[q, col, b], recv_sem=precv_sem.at[q, col],
                    device_id={"col": flip(bits[b])}, device_id_type=MESH,
                ).start()

    def passes(j, b):
        return (col % (2 * bits[b])) == (j % (2 * bits[b]))

    def receive_blocks(q, count):
        def duty(j):
            return (col != j) & passes(j, len(bits) - 1)

        @pl.loop(0, count)
        def _(j):
            @pl.when(duty(j))
            def _():
                send_block(q, j, 0).wait_recv()
                for b in reversed(range(len(bits))):
                    @pl.when(passes(j, b))
                    def _():
                        send_block(q, j, b).start()

        @pl.loop(0, count)
        def _(j):
            @pl.when((col != j) & jnp.logical_not(duty(j)))
            def _():
                send_block(q, j, 0).wait_recv()

    @pl.when(mine >= 0)
    def _():
        load_inv.start()

    @pl.loop(0, tiles)
    def _(t):
        load(0, t).start()

    for q in range(rb):
        load_own(q).start()
    for q in range(1, rb):
        @pl.loop(0, tiles)
        def _(t):
            load(q, t).start()

    barrier = pltpu.get_barrier_semaphore()
    for way in range(3):
        @pl.when(exists[way])
        def _():
            pl.semaphore_signal(barrier, inc=1, device_id={"row": targets[way]}, device_id_type=MESH)
    for bit in bits:
        pl.semaphore_signal(barrier, inc=1, device_id={"col": flip(bit)}, device_id_type=MESH)
    @pl.when(mine == 0)
    def _():
        load_inv.wait()

        @pl.loop(0, tiles)
        def _(t):
            load(0, t).wait()
            fresh = jnp.dot(
                inv[...], acc[0, t].astype(jnp.bfloat16), preferred_element_type=jnp.float32
            )
            natural[0, t] = fresh.astype(jnp.bfloat16)
            for h in range(fold):
                low[0, t * fold + h] = pack(
                    fresh if h == 0 else pltpu.roll(fresh, width - h * part, 1)
                )

    pl.semaphore_wait(
        barrier,
        1 + len(bits) + jnp.minimum(level, 1) + jnp.minimum(levels - 1 - level, 1),
    )

    @pl.when(mine == 0)
    def _():
        @pl.loop(0, chunks)
        def _(t):
            forward(0, t)

        @pl.loop(0, tiles)
        def _(t):
            store_low(0, t).start()
            store_rem(0, t).start()

    @pl.when(mine > col)
    def _():
        send_own(0)

    @pl.when(mine <= col)
    def _():
        load_own(0).wait()

    def send_later():
        for q in range(1, rb):
            send_own(q)

    @pl.when(mine <= 0)
    def _():
        send_later()

    early = (mine >= 1) & (col >= mine) & (col >= n_cols // 2)
    half = chunks // 2

    @pl.when(early)
    def _():
        @pl.loop(0, half)
        def _(p):
            send_piece(p)

    @pl.when(mine != 0)
    def _():
        @pl.loop(0, tiles)
        def _(t):
            load(0, t).wait()

    def produce(t):
        tile, h = t // fold, t % fold

        @pl.when((h == 0) & (side == 0))
        def _():
            @pl.loop(0, inv_index - 1)
            def _(j):
                acc[0, tile] -= jnp.dot(
                    lower[0, j], natural[j, tile], preferred_element_type=jnp.float32
                )

        base = turn(acc[0, tile], -h * part)
        prev = inv_index - 1
        base = base - jnp.dot(
            lower[0, prev], spread(low[prev, t]), preferred_element_type=jnp.float32
        )
        low[inv_index, t] = pack(
            jnp.dot(inv[...], base.astype(jnp.bfloat16), preferred_element_type=jnp.float32)
        )
        forward(inv_index, t)
        group = lax.broadcasted_iota(jnp.int32, (block, width), 1) // part
        acc[0, tile] = jnp.where(group == h, turn(base, h * part), acc[0, tile])

        @pl.when(h == fold - 1)
        def _():
            store_rem(0, tile).start()
            unpack(inv_index, tile)

    @pl.when(mine >= 1)
    def _():
        load_inv.wait()

    @pl.when(mine < 0)
    def _():
        @pl.loop(0, tiles)
        def _(t):
            store_rem(0, t).start()

    last = steps - 1 - side
    gather_at = last * chunks

    def gather():
        for q in range(1, rb):
            receive_blocks(q, n_cols)

            @pl.loop(0, tiles)
            def _(u):
                load(q, u).wait()

    def update(tile, start, stop):
        for q in range(1, rb):
            @pl.loop(start, stop)
            def _(j):
                acc[q, tile] -= jnp.dot(
                    lower[q, j], natural[j, tile], preferred_element_type=jnp.float32
                )

    @pl.loop(0, steps * chunks)
    def _(e):
        inner = e % (2 * chunks)
        k_plain, t_plain = e // chunks, e % chunks
        k_pair, t_pair = 2 * (e // (2 * chunks)) + 1 - inner % 2, inner // 2
        k = k_plain + side * (k_pair - k_plain)
        t = t_plain + side * (t_pair - t_plain)

        @pl.when((e == mine * chunks) & (mine >= 1) & (side == 0))
        def _():
            @pl.loop(jnp.where(early, half, 0), chunks)
            def _(p):
                send_piece(p)

        begin = (mine + 1) * chunks
        late = (mine >= 1) & (side == 1) & (mine < steps - 1)

        @pl.when(late & jnp.logical_not(early) & (e == begin))
        def _():
            @pl.loop(0, half)
            def _(p):
                send_piece(p)

        @pl.when(late & (e > begin) & (e <= begin + chunks - half))
        def _():
            send_piece(e - begin - 1 + half)

        @pl.when((e == gather_at) & ((mine < 0) | (side == 0)))
        def _():
            gather()

            @pl.loop(0, tiles)
            def _(u):
                update(u, 0, last)

        @pl.when(mine != k)
        def _():
            send_low(0, k, t).wait_recv()
            forward(k, t)

            @pl.when(t % fold == fold - 1)
            def _():
                unpack(k, t // fold)

        @pl.when((side == 1) & (k % 2 == 0) & (k + 3 <= mine) & (t % fold == fold - 1))
        def _():
            @pl.when((k == 0) & (t == fold - 1))
            def _():
                receive_blocks(0, inv_index)

            @pl.loop(k, k + 2)
            def _(j):
                acc[0, t // fold] -= jnp.dot(
                    lower[0, j], natural[j, t // fold], preferred_element_type=jnp.float32
                )

        @pl.when(mine == k + 1)
        def _():
            @pl.when((t == 0) & ((side == 0) | (mine == 1)))
            def _():
                receive_blocks(0, inv_index)

            produce(t)

            @pl.when((mine == steps - 1) & (jnp.logical_not(early) | (t >= half)))
            def _():
                send_piece(t)

        @pl.when((k == last) & (t % fold == fold - 1) & ((mine < 0) | (side == 0)))
        def _():
            tile = t // fold
            update(tile, last, steps)
            for q in range(1, rb):
                store_rem(q, tile).start()

    @pl.when((mine >= 0) & (side == 1))
    def _():
        gather()

        @pl.loop(0, tiles)
        def _(u):
            update(u, 0, steps)
            for q in range(1, rb):
                store_rem(q, u).start()

    for k in range(steps):
        for way in range(3):
            @pl.when(goes(way, k))
            def _():
                pltpu.make_async_remote_copy(
                    src_ref=low.at[k], dst_ref=low.at[k],
                    send_sem=send_sem.at[way, k], recv_sem=recv_sem.at[k, 0],
                    device_id={"row": targets[way]}, device_id_type=MESH,
                ).wait_send()
    for q in range(rb):
        for j in range(n_cols):
            used = mine > j if q == 0 else mine >= -n_rows
            for b in range(len(bits)):
                @pl.when(used & passes(j, b))
                def _():
                    send_block(q, j, b).wait_send()
    for k in range(steps):
        pltpu.make_async_copy(natural.at[k], natural.at[k], low_sem.at[k]).wait()
    for q in range(rb):
        pltpu.make_async_copy(acc.at[q], acc.at[q], rem_sem.at[q]).wait()


def on_device(n_rows, n_cols, panel, rhs, inverse):
    rb, block = panel.shape[0], panel.shape[2]
    cols = rhs.shape[3]
    steps = inverse.shape[0]
    assert panel.shape[3] == 1 and n_cols == steps
    assert n_rows % 2 == 0 and steps % 2 == 0 and n_cols & (n_cols - 1) == 0
    width = 128 if cols % 128 == 0 else cols
    tiles = cols // width
    fold = 2
    bits = n_cols.bit_length() - 1
    dma = pltpu.SemaphoreType.DMA
    low, remainder = pl.pallas_call(
        functools.partial(kernel, n_rows, n_cols, steps),
        out_shape=(
            jax.ShapeDtypeStruct((steps, block, cols), jnp.bfloat16),
            jax.ShapeDtypeStruct((rb, block, cols), jnp.float32),
        ),
        in_specs=[pl.BlockSpec(memory_space=pltpu.HBM)] * 3,
        out_specs=(pl.BlockSpec(memory_space=pl.ANY),) * 2,
        scratch_shapes=[
            pltpu.VMEM((steps, tiles * fold, block // fold, width), jnp.bfloat16),
            pltpu.VMEM((steps, tiles, block, width), jnp.bfloat16),
            pltpu.VMEM((rb, tiles, block, width), jnp.float32),
            pltpu.VMEM((block, block), jnp.bfloat16),
            pltpu.VMEM((rb, steps, block, block), jnp.bfloat16),
            dma((rb, tiles)),
            dma((rb,)),
            dma,
            dma((steps,)),
            dma((rb,)),
            dma((3, steps)),
            dma((steps, tiles * fold)),
            dma((rb, n_cols, bits)),
            dma((rb, n_cols)),
        ],
        compiler_params=pltpu.CompilerParams(
            collective_id=0, has_side_effects=True, vmem_limit_bytes=40 * 2**20
        ),
    )(*(
        pltpu.with_memory_space_constraint(x, pltpu.HBM)
        for x in (panel.reshape(rb, block, block), rhs.reshape(rb, block, cols), inverse)
    ))
    return low.astype(jnp.float32), remainder.reshape(rhs.shape)


def solution(mesh):
    placed = (P(None, "row", None, "col", None), P(None, "row", None, "col"), P())
    return jax.shard_map(
        functools.partial(on_device, mesh.shape["row"], mesh.shape["col"]),
        mesh=mesh,
        in_specs=placed,
        out_specs=(P(None, None, "col"), P(None, "row", None, "col")),
        check_vma=False,
    )
```

```python
import functools

import jax
import jax.numpy as jnp
from jax import lax
from jax.experimental import pallas as pl
from jax.experimental.pallas import tpu as pltpu
from jax.sharding import PartitionSpec as P

MESH = pl.DeviceIdType.MESH


def kernel(
    n_rows, n_cols, steps, panel, rhs, inverse, low_out, rem_out,
    low, natural, acc, inv, lower,
    load_sem, own_sem, inv_sem, low_sem, rem_sem, send_sem, recv_sem, psend_sem, precv_sem,
):
    rb = acc.shape[0]
    tiles, block, width = acc.shape[1:]
    chunks = low.shape[1]
    fold = chunks // tiles
    part, height = width // fold, block // fold
    offset = n_rows - steps
    levels = n_rows // 2
    bits = [1 << b for b in reversed(range(n_cols.bit_length() - 1))]
    row, col = lax.axis_index("row"), lax.axis_index("col")
    level, side = row // 2, row % 2
    mine = row - offset
    inv_index = jnp.maximum(mine, 0)

    def flip(bit):
        return col + bit - 2 * bit * ((col // bit) % 2)

    targets = (row + 1 - 2 * side, row - 2, row + 2)
    exists = (level >= 0, level > 0, level < levels - 1)

    def columns(t):
        return pl.ds(pl.multiple_of(t * width, width), width)

    def load(q, t):
        return pltpu.make_async_copy(rhs.at[q, :, columns(t)], acc.at[q, t], load_sem.at[q, t])

    def load_own(q):
        return pltpu.make_async_copy(panel.at[q], lower.at[q, col], own_sem.at[q])

    load_inv = pltpu.make_async_copy(inverse.at[inv_index], inv, inv_sem)

    def store_low(k, t):
        return pltpu.make_async_copy(natural.at[k, t], low_out.at[k, :, columns(t)], low_sem.at[k])

    def store_rem(q, t):
        return pltpu.make_async_copy(acc.at[q, t], rem_out.at[q, :, columns(t)], rem_sem.at[q])

    def send_low(way, k, t, p):
        rows = pl.ds(p * (height // 2), height // 2)
        return pltpu.make_async_remote_copy(
            src_ref=low.at[k, t, rows], dst_ref=low.at[k, t, rows],
            send_sem=send_sem.at[way, k], recv_sem=recv_sem.at[k, t, p],
            device_id={"row": targets[way]}, device_id_type=MESH,
        )

    def goes(way, k):
        home = (offset + k) // 2
        same = k % 2 == side
        if way == 0:
            return same
        if way == 1:
            return same & (level > 0) & (level <= home)
        return same & (level < levels - 1) & (level >= home)

    def forward(k, t):
        for p in range(2):
            forward_half(k, t, p)

    def forward_half(k, t, p):
        for way, when in ((0, side == 0), (2, True), (1, True), (0, side == 1)):
            @pl.when(goes(way, k) & when)
            def _():
                send_low(way, k, t, p).start()

    lane = lax.broadcasted_iota(jnp.int32, (height, width), 1) // part

    def turn(x, shift):
        return pltpu.roll(x, lax.rem(shift + width, width), 1)

    def spread(p):
        wide = p.astype(jnp.float32)
        return jnp.concatenate(
            [wide] + [pltpu.roll(wide, width - g * part, 1) for g in range(1, fold)], axis=0
        ).astype(jnp.bfloat16)

    def pack(x):
        out = x[:height]
        for g in range(1, fold):
            moved = pltpu.roll(x[g * height : (g + 1) * height], g * part, 1)
            out = jnp.where(lane == g, moved, out)
        return out.astype(jnp.bfloat16)

    def unpack(k, tile):
        held = [low[k, tile * fold + h].astype(jnp.float32) for h in range(fold)]
        for g in range(fold):
            out = held[0] if g == 0 else pltpu.roll(held[0], width - g * part, 1)
            for h in range(1, fold):
                shift = (h - g) * part % width
                moved = held[h] if shift == 0 else pltpu.roll(held[h], shift, 1)
                out = jnp.where(lane == h, moved, out)
            natural[k, tile, pl.ds(g * height, height), :] = out.astype(jnp.bfloat16)
        store_low(k, tile).start()

    def send_block(q, j, b):
        return pltpu.make_async_remote_copy(
            src_ref=lower.at[q, j], dst_ref=lower.at[q, j],
            send_sem=psend_sem.at[q, j, b], recv_sem=precv_sem.at[q, j],
            device_id={"col": flip(bits[b])}, device_id_type=MESH,
        )

    def send_own(q):
        load_own(q).wait()
        for b in reversed(range(len(bits))):
            send_block(q, col, b).start()

    def send_piece(p):
        rows = pl.ds(pl.multiple_of(p * (block // chunks), block // chunks), block // chunks)
        for q in range(1, rb):
            @pl.when(p == 0)
            def _():
                load_own(q).wait()

            for b in reversed(range(len(bits))):
                pltpu.make_async_remote_copy(
                    src_ref=lower.at[q, col, rows], dst_ref=lower.at[q, col, rows],
                    send_sem=psend_sem.at[q, col, b], recv_sem=precv_sem.at[q, col],
                    device_id={"col": flip(bits[b])}, device_id_type=MESH,
                ).start()

    def passes(j, b):
        return (col % (2 * bits[b])) == (j % (2 * bits[b]))

    def receive_blocks(q, count):
        def duty(j):
            return (col != j) & passes(j, len(bits) - 1)

        @pl.loop(0, count)
        def _(j):
            @pl.when(duty(j))
            def _():
                send_block(q, j, 0).wait_recv()
                for b in reversed(range(len(bits))):
                    @pl.when(passes(j, b))
                    def _():
                        send_block(q, j, b).start()

        @pl.loop(0, count)
        def _(j):
            @pl.when((col != j) & jnp.logical_not(duty(j)))
            def _():
                send_block(q, j, 0).wait_recv()

    @pl.when(mine >= 0)
    def _():
        load_inv.start()

    @pl.loop(0, tiles)
    def _(t):
        load(0, t).start()

    for q in range(rb):
        load_own(q).start()
    for q in range(1, rb):
        @pl.loop(0, tiles)
        def _(t):
            load(q, t).start()

    barrier = pltpu.get_barrier_semaphore()
    for way in range(3):
        @pl.when(exists[way])
        def _():
            pl.semaphore_signal(barrier, inc=1, device_id={"row": targets[way]}, device_id_type=MESH)
    for bit in bits:
        pl.semaphore_signal(barrier, inc=1, device_id={"col": flip(bit)}, device_id_type=MESH)
    def solve_first(t):
        load(0, t).wait()
        fresh = jnp.dot(
            inv[...], acc[0, t].astype(jnp.bfloat16), preferred_element_type=jnp.float32
        )
        natural[0, t] = fresh.astype(jnp.bfloat16)
        for h in range(fold):
            low[0, t * fold + h] = pack(
                fresh if h == 0 else pltpu.roll(fresh, width - h * part, 1)
            )

    @pl.when(mine == 0)
    def _():
        load_inv.wait()
        solve_first(0)

    pl.semaphore_wait(
        barrier,
        1 + len(bits) + jnp.minimum(level, 1) + jnp.minimum(levels - 1 - level, 1),
    )

    @pl.when(mine == 0)
    def _():
        @pl.loop(0, tiles)
        def _(t):
            @pl.when(t > 0)
            def _():
                solve_first(t)

            for h in range(fold):
                forward(0, t * fold + h)
            store_low(0, t).start()
            store_rem(0, t).start()

    @pl.when(mine > col)
    def _():
        send_own(0)

    @pl.when(mine <= col)
    def _():
        load_own(0).wait()

    def send_later():
        for q in range(1, rb):
            send_own(q)

    @pl.when(mine <= 0)
    def _():
        send_later()

    early = (mine >= 1) & (col >= mine) & (col >= n_cols // 2)
    half = chunks // 2

    @pl.when(early)
    def _():
        @pl.loop(0, half)
        def _(p):
            send_piece(p)

    @pl.when(mine != 0)
    def _():
        @pl.loop(0, tiles)
        def _(t):
            load(0, t).wait()

    def produce(t):
        tile, h = t // fold, t % fold

        @pl.when((h == 0) & (side == 0))
        def _():
            @pl.loop(0, inv_index - 1)
            def _(j):
                acc[0, tile] -= jnp.dot(
                    lower[0, j], natural[j, tile], preferred_element_type=jnp.float32
                )

        base = turn(acc[0, tile], -h * part)
        prev = inv_index - 1
        base = base - jnp.dot(
            lower[0, prev], spread(low[prev, t]), preferred_element_type=jnp.float32
        )
        low[inv_index, t] = pack(
            jnp.dot(inv[...], base.astype(jnp.bfloat16), preferred_element_type=jnp.float32)
        )
        forward(inv_index, t)
        group = lax.broadcasted_iota(jnp.int32, (block, width), 1) // part
        acc[0, tile] = jnp.where(group == h, turn(base, h * part), acc[0, tile])

        @pl.when(h == fold - 1)
        def _():
            store_rem(0, tile).start()
            unpack(inv_index, tile)

    @pl.when(mine >= 1)
    def _():
        load_inv.wait()

    @pl.when(mine < 0)
    def _():
        @pl.loop(0, tiles)
        def _(t):
            store_rem(0, t).start()

    last = steps - 1 - side
    gather_at = last * chunks

    def gather():
        for q in range(1, rb):
            receive_blocks(q, n_cols)

            @pl.loop(0, tiles)
            def _(u):
                load(q, u).wait()

    def update(tile, start, stop):
        for q in range(1, rb):
            @pl.loop(start, stop)
            def _(j):
                acc[q, tile] -= jnp.dot(
                    lower[q, j], natural[j, tile], preferred_element_type=jnp.float32
                )

    @pl.loop(0, steps * chunks)
    def _(e):
        inner = e % (2 * chunks)
        k_plain, t_plain = e // chunks, e % chunks
        k_pair, t_pair = 2 * (e // (2 * chunks)) + 1 - inner % 2, inner // 2
        k = k_plain + side * (k_pair - k_plain)
        t = t_plain + side * (t_pair - t_plain)

        @pl.when((e == mine * chunks) & (mine >= 1) & (side == 0))
        def _():
            @pl.loop(jnp.where(early, half, 0), chunks)
            def _(p):
                send_piece(p)

        begin = (mine + 1) * chunks
        late = (mine >= 1) & (side == 1) & (mine < steps - 1)

        @pl.when(late & jnp.logical_not(early) & (e == begin))
        def _():
            @pl.loop(0, half)
            def _(p):
                send_piece(p)

        @pl.when(late & (e > begin) & (e <= begin + chunks - half))
        def _():
            send_piece(e - begin - 1 + half)

        @pl.when((e == gather_at) & ((mine < 0) | (side == 0)))
        def _():
            gather()

            @pl.loop(0, tiles)
            def _(u):
                update(u, 0, last)

        @pl.when(mine != k)
        def _():
            for p in range(2):
                send_low(0, k, t, p).wait_recv()
                forward_half(k, t, p)

            @pl.when(t % fold == fold - 1)
            def _():
                unpack(k, t // fold)

        @pl.when((side == 1) & (k % 2 == 0) & (k + 3 <= mine) & (t % fold == fold - 1))
        def _():
            @pl.when((k == 0) & (t == fold - 1))
            def _():
                receive_blocks(0, inv_index)

            @pl.loop(k, k + 2)
            def _(j):
                acc[0, t // fold] -= jnp.dot(
                    lower[0, j], natural[j, t // fold], preferred_element_type=jnp.float32
                )

        @pl.when(mine == k + 1)
        def _():
            @pl.when((t == 0) & ((side == 0) | (mine == 1)))
            def _():
                receive_blocks(0, inv_index)

            produce(t)

            @pl.when((mine == steps - 1) & (jnp.logical_not(early) | (t >= half)))
            def _():
                send_piece(t)

        @pl.when((k == last) & (t % fold == fold - 1) & ((mine < 0) | (side == 0)))
        def _():
            tile = t // fold
            update(tile, last, steps)
            for q in range(1, rb):
                store_rem(q, tile).start()

    @pl.when((mine >= 0) & (side == 1))
    def _():
        gather()

        @pl.loop(0, tiles)
        def _(u):
            update(u, 0, steps)
            for q in range(1, rb):
                store_rem(q, u).start()

    for k in range(steps):
        for way in range(3):
            @pl.when(goes(way, k))
            def _():
                pltpu.make_async_remote_copy(
                    src_ref=low.at[k], dst_ref=low.at[k],
                    send_sem=send_sem.at[way, k], recv_sem=recv_sem.at[k, 0, 0],
                    device_id={"row": targets[way]}, device_id_type=MESH,
                ).wait_send()
    for q in range(rb):
        for j in range(n_cols):
            used = mine > j if q == 0 else mine >= -n_rows
            for b in range(len(bits)):
                @pl.when(used & passes(j, b))
                def _():
                    send_block(q, j, b).wait_send()
    for k in range(steps):
        pltpu.make_async_copy(natural.at[k], natural.at[k], low_sem.at[k]).wait()
    for q in range(rb):
        pltpu.make_async_copy(acc.at[q], acc.at[q], rem_sem.at[q]).wait()


def on_device(n_rows, n_cols, panel, rhs, inverse):
    rb, block = panel.shape[0], panel.shape[2]
    cols = rhs.shape[3]
    steps = inverse.shape[0]
    assert panel.shape[3] == 1 and n_cols == steps
    assert n_rows % 2 == 0 and steps % 2 == 0 and n_cols & (n_cols - 1) == 0
    width = 128 if cols % 128 == 0 else cols
    tiles = cols // width
    fold = 2
    bits = n_cols.bit_length() - 1
    dma = pltpu.SemaphoreType.DMA
    low, remainder = pl.pallas_call(
        functools.partial(kernel, n_rows, n_cols, steps),
        out_shape=(
            jax.ShapeDtypeStruct((steps, block, cols), jnp.bfloat16),
            jax.ShapeDtypeStruct((rb, block, cols), jnp.float32),
        ),
        in_specs=[pl.BlockSpec(memory_space=pltpu.HBM)] * 3,
        out_specs=(pl.BlockSpec(memory_space=pl.ANY),) * 2,
        scratch_shapes=[
            pltpu.VMEM((steps, tiles * fold, block // fold, width), jnp.bfloat16),
            pltpu.VMEM((steps, tiles, block, width), jnp.bfloat16),
            pltpu.VMEM((rb, tiles, block, width), jnp.float32),
            pltpu.VMEM((block, block), jnp.bfloat16),
            pltpu.VMEM((rb, steps, block, block), jnp.bfloat16),
            dma((rb, tiles)),
            dma((rb,)),
            dma,
            dma((steps,)),
            dma((rb,)),
            dma((3, steps)),
            dma((steps, tiles * fold, 2)),
            dma((rb, n_cols, bits)),
            dma((rb, n_cols)),
        ],
        compiler_params=pltpu.CompilerParams(
            collective_id=0, has_side_effects=True, vmem_limit_bytes=40 * 2**20
        ),
    )(*(
        pltpu.with_memory_space_constraint(x, pltpu.HBM)
        for x in (panel.reshape(rb, block, block), rhs.reshape(rb, block, cols), inverse)
    ))
    return low.astype(jnp.float32), remainder.reshape(rhs.shape)


def solution(mesh):
    placed = (P(None, "row", None, "col", None), P(None, "row", None, "col"), P())
    return jax.shard_map(
        functools.partial(on_device, mesh.shape["row"], mesh.shape["col"]),
        mesh=mesh,
        in_specs=placed,
        out_specs=(P(None, None, "col"), P(None, "row", None, "col")),
        check_vma=False,
    )
```

```python
import functools

import jax
import jax.numpy as jnp
from jax import lax
from jax.experimental import pallas as pl
from jax.experimental.pallas import tpu as pltpu
from jax.sharding import PartitionSpec as P

MESH = pl.DeviceIdType.MESH


def kernel(
    n_rows, n_cols, steps, panel, rhs, inverse, low_out, rem_out,
    low, natural, acc, inv, lower,
    load_sem, own_sem, inv_sem, low_sem, rem_sem, send_sem, recv_sem, psend_sem, precv_sem,
):
    rb = acc.shape[0]
    tiles, block, width = acc.shape[1:]
    chunks = low.shape[1]
    fold = chunks // tiles
    part, height = width // fold, block // fold
    offset = n_rows - steps
    levels = n_rows // 2
    bits = [1 << b for b in reversed(range(n_cols.bit_length() - 1))]
    row, col = lax.axis_index("row"), lax.axis_index("col")
    level, side = row // 2, row % 2
    mine = row - offset
    inv_index = jnp.maximum(mine, 0)

    def flip(bit):
        return col + bit - 2 * bit * ((col // bit) % 2)

    targets = (row + 1 - 2 * side, row - 2, row + 2)
    exists = (level >= 0, level > 0, level < levels - 1)

    def columns(t):
        return pl.ds(pl.multiple_of(t * width, width), width)

    def load(q, t):
        return pltpu.make_async_copy(rhs.at[q, :, columns(t)], acc.at[q, t], load_sem.at[q, t])

    def load_own(q):
        return pltpu.make_async_copy(panel.at[q], lower.at[q, col], own_sem.at[q])

    load_inv = pltpu.make_async_copy(inverse.at[inv_index], inv, inv_sem)

    def store_low(k, t):
        return pltpu.make_async_copy(natural.at[k, t], low_out.at[k, :, columns(t)], low_sem.at[k])

    def store_rem(q, t):
        return pltpu.make_async_copy(acc.at[q, t], rem_out.at[q, :, columns(t)], rem_sem.at[q])

    def send_low(way, k, t, p):
        rows = pl.ds(p * (height // 2), height // 2)
        return pltpu.make_async_remote_copy(
            src_ref=low.at[k, t, rows], dst_ref=low.at[k, t, rows],
            send_sem=send_sem.at[way, k], recv_sem=recv_sem.at[k, t, p],
            device_id={"row": targets[way]}, device_id_type=MESH,
        )

    def goes(way, k):
        home = (offset + k) // 2
        same = k % 2 == side
        if way == 0:
            return same
        if way == 1:
            return same & (level > 0) & (level <= home)
        return same & (level < levels - 1) & (level >= home)

    def forward(k, t):
        for p in range(2):
            forward_half(k, t, p)

    def forward_half(k, t, p):
        for way, when in ((0, side == 0), (2, True), (1, True), (0, side == 1)):
            @pl.when(goes(way, k) & when)
            def _():
                send_low(way, k, t, p).start()

    lane = lax.broadcasted_iota(jnp.int32, (height, width), 1) // part

    def turn(x, shift):
        return pltpu.roll(x, lax.rem(shift + width, width), 1)

    def spread(p):
        wide = p.astype(jnp.float32)
        return jnp.concatenate(
            [wide] + [pltpu.roll(wide, width - g * part, 1) for g in range(1, fold)], axis=0
        ).astype(jnp.bfloat16)

    def pack(x):
        out = x[:height]
        for g in range(1, fold):
            moved = pltpu.roll(x[g * height : (g + 1) * height], g * part, 1)
            out = jnp.where(lane == g, moved, out)
        return out.astype(jnp.bfloat16)

    def unpack(k, tile):
        held = [low[k, tile * fold + h].astype(jnp.float32) for h in range(fold)]
        for g in range(fold):
            out = held[0] if g == 0 else pltpu.roll(held[0], width - g * part, 1)
            for h in range(1, fold):
                shift = (h - g) * part % width
                moved = held[h] if shift == 0 else pltpu.roll(held[h], shift, 1)
                out = jnp.where(lane == h, moved, out)
            natural[k, tile, pl.ds(g * height, height), :] = out.astype(jnp.bfloat16)
        store_low(k, tile).start()

    def send_block(q, j, b):
        return pltpu.make_async_remote_copy(
            src_ref=lower.at[q, j], dst_ref=lower.at[q, j],
            send_sem=psend_sem.at[q, j, b], recv_sem=precv_sem.at[q, j],
            device_id={"col": flip(bits[b])}, device_id_type=MESH,
        )

    def send_own(q):
        load_own(q).wait()
        for b in reversed(range(len(bits))):
            send_block(q, col, b).start()

    def send_piece(p):
        rows = pl.ds(pl.multiple_of(p * (block // chunks), block // chunks), block // chunks)
        for q in range(1, rb):
            @pl.when(p == 0)
            def _():
                load_own(q).wait()

            for b in reversed(range(len(bits))):
                pltpu.make_async_remote_copy(
                    src_ref=lower.at[q, col, rows], dst_ref=lower.at[q, col, rows],
                    send_sem=psend_sem.at[q, col, b], recv_sem=precv_sem.at[q, col],
                    device_id={"col": flip(bits[b])}, device_id_type=MESH,
                ).start()

    def passes(j, b):
        return (col % (2 * bits[b])) == (j % (2 * bits[b]))

    def receive_blocks(q, count):
        def duty(j):
            return (col != j) & passes(j, len(bits) - 1)

        @pl.loop(0, count)
        def _(j):
            @pl.when(duty(j))
            def _():
                send_block(q, j, 0).wait_recv()
                for b in reversed(range(len(bits))):
                    @pl.when(passes(j, b))
                    def _():
                        send_block(q, j, b).start()

        @pl.loop(0, count)
        def _(j):
            @pl.when((col != j) & jnp.logical_not(duty(j)))
            def _():
                send_block(q, j, 0).wait_recv()

    @pl.when(mine >= 0)
    def _():
        load_inv.start()

    @pl.loop(0, tiles)
    def _(t):
        load(0, t).start()

    for q in range(rb):
        load_own(q).start()
    for q in range(1, rb):
        @pl.loop(0, tiles)
        def _(t):
            load(q, t).start()

    barrier = pltpu.get_barrier_semaphore()
    for way in range(3):
        @pl.when(exists[way])
        def _():
            pl.semaphore_signal(barrier, inc=1, device_id={"row": targets[way]}, device_id_type=MESH)
    for bit in bits:
        pl.semaphore_signal(barrier, inc=1, device_id={"col": flip(bit)}, device_id_type=MESH)
    def solve_first(t):
        load(0, t).wait()
        fresh = jnp.dot(
            inv[...], acc[0, t].astype(jnp.bfloat16), preferred_element_type=jnp.float32
        )
        natural[0, t] = fresh.astype(jnp.bfloat16)
        for h in range(fold):
            low[0, t * fold + h] = pack(
                fresh if h == 0 else pltpu.roll(fresh, width - h * part, 1)
            )

    @pl.when(mine == 0)
    def _():
        load_inv.wait()
        solve_first(0)

    pl.semaphore_wait(
        barrier,
        1 + len(bits) + jnp.minimum(level, 1) + jnp.minimum(levels - 1 - level, 1),
    )

    @pl.when(mine == 0)
    def _():
        @pl.loop(0, tiles)
        def _(t):
            @pl.when(t > 0)
            def _():
                solve_first(t)

            for h in range(fold):
                forward(0, t * fold + h)
            store_low(0, t).start()
            store_rem(0, t).start()

    @pl.when(mine > col)
    def _():
        send_own(0)

    @pl.when(mine <= col)
    def _():
        load_own(0).wait()

    def send_later():
        for q in range(1, rb):
            send_own(q)

    @pl.when(mine <= 0)
    def _():
        send_later()

    early = (mine >= 1) & (col >= mine) & (col >= n_cols // 2)
    half = chunks // 2

    @pl.when(early)
    def _():
        @pl.loop(0, half)
        def _(p):
            send_piece(p)

    @pl.when(mine != 0)
    def _():
        @pl.loop(0, tiles)
        def _(t):
            load(0, t).wait()

    def produce(t):
        tile, h = t // fold, t % fold

        @pl.when((h == 0) & (side == 0))
        def _():
            @pl.loop(0, inv_index - 1)
            def _(j):
                acc[0, tile] -= jnp.dot(
                    lower[0, j], natural[j, tile], preferred_element_type=jnp.float32
                )

        base = turn(acc[0, tile], -h * part)
        prev = inv_index - 1
        base = base - jnp.dot(
            lower[0, prev], spread(low[prev, t]), preferred_element_type=jnp.float32
        )
        low[inv_index, t] = pack(
            jnp.dot(inv[...], base.astype(jnp.bfloat16), preferred_element_type=jnp.float32)
        )
        forward(inv_index, t)
        group = lax.broadcasted_iota(jnp.int32, (block, width), 1) // part
        acc[0, tile] = jnp.where(group == h, turn(base, h * part), acc[0, tile])

        @pl.when(h == fold - 1)
        def _():
            store_rem(0, tile).start()
            unpack(inv_index, tile)

    @pl.when(mine >= 1)
    def _():
        load_inv.wait()

    @pl.when(mine < 0)
    def _():
        @pl.loop(0, tiles)
        def _(t):
            store_rem(0, t).start()

    last = steps - 1 - side
    first = steps - 2
    gather_at = first * chunks

    def gather():
        for q in range(1, rb):
            receive_blocks(q, n_cols)

            @pl.loop(0, tiles)
            def _(u):
                load(q, u).wait()

    def update(tile, start, stop):
        for q in range(1, rb):
            @pl.loop(start, stop)
            def _(j):
                acc[q, tile] -= jnp.dot(
                    lower[q, j], natural[j, tile], preferred_element_type=jnp.float32
                )

    @pl.loop(0, steps * chunks)
    def _(e):
        inner = e % (2 * chunks)
        k_plain, t_plain = e // chunks, e % chunks
        k_pair, t_pair = 2 * (e // (2 * chunks)) + 1 - inner % 2, inner // 2
        k = k_plain + side * (k_pair - k_plain)
        t = t_plain + side * (t_pair - t_plain)

        @pl.when((e == mine * chunks) & (mine >= 1) & (side == 0))
        def _():
            @pl.loop(jnp.where(early, half, 0), chunks)
            def _(p):
                send_piece(p)

        begin = (mine + 1) * chunks
        late = (mine >= 1) & (side == 1) & (mine < steps - 1)

        @pl.when(late & jnp.logical_not(early) & (e == begin))
        def _():
            @pl.loop(0, half)
            def _(p):
                send_piece(p)

        @pl.when(late & (e > begin) & (e <= begin + chunks - half))
        def _():
            send_piece(e - begin - 1 + half)

        @pl.when((e == gather_at) & ((mine < 0) | (side == 0)))
        def _():
            gather()

            @pl.loop(0, tiles)
            def _(u):
                update(u, 0, first)

        @pl.when(mine != k)
        def _():
            for p in range(2):
                send_low(0, k, t, p).wait_recv()
                forward_half(k, t, p)

            @pl.when(t % fold == fold - 1)
            def _():
                unpack(k, t // fold)

        @pl.when((side == 1) & (k % 2 == 0) & (k + 3 <= mine) & (t % fold == fold - 1))
        def _():
            @pl.when((k == 0) & (t == fold - 1))
            def _():
                receive_blocks(0, inv_index)

            @pl.loop(k, k + 2)
            def _(j):
                acc[0, t // fold] -= jnp.dot(
                    lower[0, j], natural[j, t // fold], preferred_element_type=jnp.float32
                )

        @pl.when(mine == k + 1)
        def _():
            @pl.when((t == 0) & ((side == 0) | (mine == 1)))
            def _():
                receive_blocks(0, inv_index)

            produce(t)

            @pl.when((mine == steps - 1) & (jnp.logical_not(early) | (t >= half)))
            def _():
                send_piece(t)

        @pl.when(
            (k >= first) & ((side == 0) | ((k == last) & (mine < 0))) & (t % fold == fold - 1)
        )
        def _():
            tile = t // fold
            update(tile, first + (1 - side) * (k - first), steps - (1 - side) * (steps - 1 - k))

            @pl.when(k == last)
            def _():
                for q in range(1, rb):
                    store_rem(q, tile).start()

    @pl.when((mine >= 0) & (side == 1))
    def _():
        gather()

        @pl.loop(0, tiles)
        def _(u):
            update(u, 0, steps)
            for q in range(1, rb):
                store_rem(q, u).start()

    for k in range(steps):
        for way in range(3):
            @pl.when(goes(way, k))
            def _():
                pltpu.make_async_remote_copy(
                    src_ref=low.at[k], dst_ref=low.at[k],
                    send_sem=send_sem.at[way, k], recv_sem=recv_sem.at[k, 0, 0],
                    device_id={"row": targets[way]}, device_id_type=MESH,
                ).wait_send()
    for q in range(rb):
        for j in range(n_cols):
            used = mine > j if q == 0 else mine >= -n_rows
            for b in range(len(bits)):
                @pl.when(used & passes(j, b))
                def _():
                    send_block(q, j, b).wait_send()
    for k in range(steps):
        pltpu.make_async_copy(natural.at[k], natural.at[k], low_sem.at[k]).wait()
    for q in range(rb):
        pltpu.make_async_copy(acc.at[q], acc.at[q], rem_sem.at[q]).wait()


def on_device(n_rows, n_cols, panel, rhs, inverse):
    rb, block = panel.shape[0], panel.shape[2]
    cols = rhs.shape[3]
    steps = inverse.shape[0]
    assert panel.shape[3] == 1 and n_cols == steps
    assert n_rows % 2 == 0 and steps % 2 == 0 and n_cols & (n_cols - 1) == 0
    width = 128 if cols % 128 == 0 else cols
    tiles = cols // width
    fold = 2
    bits = n_cols.bit_length() - 1
    dma = pltpu.SemaphoreType.DMA
    low, remainder = pl.pallas_call(
        functools.partial(kernel, n_rows, n_cols, steps),
        out_shape=(
            jax.ShapeDtypeStruct((steps, block, cols), jnp.bfloat16),
            jax.ShapeDtypeStruct((rb, block, cols), jnp.float32),
        ),
        in_specs=[pl.BlockSpec(memory_space=pltpu.HBM)] * 3,
        out_specs=(pl.BlockSpec(memory_space=pl.ANY),) * 2,
        scratch_shapes=[
            pltpu.VMEM((steps, tiles * fold, block // fold, width), jnp.bfloat16),
            pltpu.VMEM((steps, tiles, block, width), jnp.bfloat16),
            pltpu.VMEM((rb, tiles, block, width), jnp.float32),
            pltpu.VMEM((block, block), jnp.bfloat16),
            pltpu.VMEM((rb, steps, block, block), jnp.bfloat16),
            dma((rb, tiles)),
            dma((rb,)),
            dma,
            dma((steps,)),
            dma((rb,)),
            dma((3, steps)),
            dma((steps, tiles * fold, 2)),
            dma((rb, n_cols, bits)),
            dma((rb, n_cols)),
        ],
        compiler_params=pltpu.CompilerParams(
            collective_id=0, has_side_effects=True, vmem_limit_bytes=40 * 2**20
        ),
    )(*(
        pltpu.with_memory_space_constraint(x, pltpu.HBM)
        for x in (panel.reshape(rb, block, block), rhs.reshape(rb, block, cols), inverse)
    ))
    return low.astype(jnp.float32), remainder.reshape(rhs.shape)


def solution(mesh):
    placed = (P(None, "row", None, "col", None), P(None, "row", None, "col"), P())
    return jax.shard_map(
        functools.partial(on_device, mesh.shape["row"], mesh.shape["col"]),
        mesh=mesh,
        in_specs=placed,
        out_specs=(P(None, None, "col"), P(None, "row", None, "col")),
        check_vma=False,
    )
```

```python
import functools

import jax
import jax.numpy as jnp
from jax import lax
from jax.experimental import pallas as pl
from jax.experimental.pallas import tpu as pltpu
from jax.sharding import PartitionSpec as P

MESH = pl.DeviceIdType.MESH


def kernel(
    n_rows, n_cols, steps, panel, rhs, inverse, low_out, rem_out,
    low, natural, acc, inv, lower,
    load_sem, own_sem, inv_sem, low_sem, rem_sem, send_sem, recv_sem, psend_sem, precv_sem,
):
    rb = acc.shape[0]
    tiles, block, width = acc.shape[1:]
    chunks = low.shape[1]
    fold = chunks // tiles
    part, height = width // fold, block // fold
    offset = n_rows - steps
    levels = n_rows // 2
    bits = [1 << b for b in reversed(range(n_cols.bit_length() - 1))]
    row, col = lax.axis_index("row"), lax.axis_index("col")
    level, side = row // 2, row % 2
    mine = row - offset
    inv_index = jnp.maximum(mine, 0)

    def flip(bit):
        return col + bit - 2 * bit * ((col // bit) % 2)

    targets = (row + 1 - 2 * side, row - 2, row + 2)
    exists = (level >= 0, level > 0, level < levels - 1)

    def columns(t):
        return pl.ds(pl.multiple_of(t * width, width), width)

    def load(q, t):
        return pltpu.make_async_copy(rhs.at[q, :, columns(t)], acc.at[q, t], load_sem.at[q, t])

    def load_own(q):
        return pltpu.make_async_copy(panel.at[q], lower.at[q, col], own_sem.at[q])

    load_inv = pltpu.make_async_copy(inverse.at[inv_index], inv, inv_sem)

    def store_low(k, t):
        return pltpu.make_async_copy(natural.at[k, t], low_out.at[k, :, columns(t)], low_sem.at[k])

    def store_rem(q, t):
        return pltpu.make_async_copy(acc.at[q, t], rem_out.at[q, :, columns(t)], rem_sem.at[q])

    def send_low(way, k, t, p):
        rows = pl.ds(p * (height // 2), height // 2)
        return pltpu.make_async_remote_copy(
            src_ref=low.at[k, t, rows], dst_ref=low.at[k, t, rows],
            send_sem=send_sem.at[way, k], recv_sem=recv_sem.at[k, t, p],
            device_id={"row": targets[way]}, device_id_type=MESH,
        )

    def goes(way, k):
        home = (offset + k) // 2
        same = k % 2 == side
        if way == 0:
            return same
        if way == 1:
            return same & (level > 0) & (level <= home)
        return same & (level < levels - 1) & (level >= home)

    def forward(k, t):
        for p in range(2):
            forward_half(k, t, p)

    def forward_half(k, t, p):
        for way, when in ((0, side == 0), (2, True), (1, True), (0, side == 1)):
            @pl.when(goes(way, k) & when)
            def _():
                send_low(way, k, t, p).start()

    lane = lax.broadcasted_iota(jnp.int32, (height, width), 1) // part

    def turn(x, shift):
        return pltpu.roll(x, lax.rem(shift + width, width), 1)

    def spread(p):
        wide = p.astype(jnp.float32)
        return jnp.concatenate(
            [wide] + [pltpu.roll(wide, width - g * part, 1) for g in range(1, fold)], axis=0
        ).astype(jnp.bfloat16)

    def pack(x):
        out = x[:height]
        for g in range(1, fold):
            moved = pltpu.roll(x[g * height : (g + 1) * height], g * part, 1)
            out = jnp.where(lane == g, moved, out)
        return out.astype(jnp.bfloat16)

    def unpack(k, tile):
        held = [low[k, tile * fold + h].astype(jnp.float32) for h in range(fold)]
        for g in range(fold):
            out = held[0] if g == 0 else pltpu.roll(held[0], width - g * part, 1)
            for h in range(1, fold):
                shift = (h - g) * part % width
                moved = held[h] if shift == 0 else pltpu.roll(held[h], shift, 1)
                out = jnp.where(lane == h, moved, out)
            natural[k, tile, pl.ds(g * height, height), :] = out.astype(jnp.bfloat16)
        store_low(k, tile).start()

    def send_block(q, j, b):
        return pltpu.make_async_remote_copy(
            src_ref=lower.at[q, j], dst_ref=lower.at[q, j],
            send_sem=psend_sem.at[q, j, b], recv_sem=precv_sem.at[q, j],
            device_id={"col": flip(bits[b])}, device_id_type=MESH,
        )

    def send_own(q):
        load_own(q).wait()
        for b in reversed(range(len(bits))):
            send_block(q, col, b).start()

    def send_piece(p):
        rows = pl.ds(pl.multiple_of(p * (block // chunks), block // chunks), block // chunks)
        for q in range(1, rb):
            @pl.when(p == 0)
            def _():
                load_own(q).wait()

            for b in reversed(range(len(bits))):
                pltpu.make_async_remote_copy(
                    src_ref=lower.at[q, col, rows], dst_ref=lower.at[q, col, rows],
                    send_sem=psend_sem.at[q, col, b], recv_sem=precv_sem.at[q, col],
                    device_id={"col": flip(bits[b])}, device_id_type=MESH,
                ).start()

    def passes(j, b):
        return (col % (2 * bits[b])) == (j % (2 * bits[b]))

    def receive_blocks(q, count):
        def duty(j):
            return (col != j) & passes(j, len(bits) - 1)

        @pl.loop(0, count)
        def _(j):
            @pl.when(duty(j))
            def _():
                send_block(q, j, 0).wait_recv()
                for b in reversed(range(len(bits))):
                    @pl.when(passes(j, b))
                    def _():
                        send_block(q, j, b).start()

        @pl.loop(0, count)
        def _(j):
            @pl.when((col != j) & jnp.logical_not(duty(j)))
            def _():
                send_block(q, j, 0).wait_recv()

    @pl.when(mine >= 0)
    def _():
        load_inv.start()

    @pl.loop(0, tiles)
    def _(t):
        load(0, t).start()

    for q in range(rb):
        load_own(q).start()
    for q in range(1, rb):
        @pl.loop(0, tiles)
        def _(t):
            load(q, t).start()

    barrier = pltpu.get_barrier_semaphore()
    for way in range(3):
        @pl.when(exists[way])
        def _():
            pl.semaphore_signal(barrier, inc=1, device_id={"row": targets[way]}, device_id_type=MESH)
    for bit in bits:
        pl.semaphore_signal(barrier, inc=1, device_id={"col": flip(bit)}, device_id_type=MESH)
    def solve_first(t):
        load(0, t).wait()
        fresh = jnp.dot(
            inv[...], acc[0, t].astype(jnp.bfloat16), preferred_element_type=jnp.float32
        )
        natural[0, t] = fresh.astype(jnp.bfloat16)
        for h in range(fold):
            low[0, t * fold + h] = pack(
                fresh if h == 0 else pltpu.roll(fresh, width - h * part, 1)
            )

    @pl.when(mine == 0)
    def _():
        load_inv.wait()
        solve_first(0)

    pl.semaphore_wait(
        barrier,
        1 + len(bits) + jnp.minimum(level, 1) + jnp.minimum(levels - 1 - level, 1),
    )

    @pl.when(mine == 0)
    def _():
        @pl.loop(0, tiles)
        def _(t):
            @pl.when(t > 0)
            def _():
                solve_first(t)

            for h in range(fold):
                forward(0, t * fold + h)
            store_low(0, t).start()
            store_rem(0, t).start()

    @pl.when(mine > col)
    def _():
        send_own(0)

    @pl.when(mine <= col)
    def _():
        load_own(0).wait()

    def send_later():
        for q in range(1, rb):
            send_own(q)

    @pl.when(mine <= 0)
    def _():
        send_later()

    early = (mine >= 1) & (col >= mine) & (col >= n_cols // 2)
    half = chunks // 2

    @pl.when(early)
    def _():
        @pl.loop(0, half)
        def _(p):
            send_piece(p)

    @pl.when(mine != 0)
    def _():
        @pl.loop(0, tiles)
        def _(t):
            load(0, t).wait()

    def produce(t):
        tile, h = t // fold, t % fold

        @pl.when((h == 0) & (side == 0))
        def _():
            @pl.loop(0, inv_index - 1)
            def _(j):
                acc[0, tile] -= jnp.dot(
                    lower[0, j], natural[j, tile], preferred_element_type=jnp.float32
                )

        base = turn(acc[0, tile], -h * part)
        prev = inv_index - 1
        base = base - jnp.dot(
            lower[0, prev], spread(low[prev, t]), preferred_element_type=jnp.float32
        )
        low[inv_index, t] = pack(
            jnp.dot(inv[...], base.astype(jnp.bfloat16), preferred_element_type=jnp.float32)
        )
        forward(inv_index, t)
        group = lax.broadcasted_iota(jnp.int32, (block, width), 1) // part
        acc[0, tile] = jnp.where(group == h, turn(base, h * part), acc[0, tile])

        @pl.when(h == fold - 1)
        def _():
            store_rem(0, tile).start()
            unpack(inv_index, tile)

    @pl.when(mine >= 1)
    def _():
        load_inv.wait()

    @pl.when(mine < 0)
    def _():
        @pl.loop(0, tiles)
        def _(t):
            store_rem(0, t).start()

    ahead = min(2, chunks)
    last = steps - 1 - side
    gather_at = last * chunks

    def gather():
        for q in range(1, rb):
            receive_blocks(q, n_cols)

            @pl.loop(0, tiles)
            def _(u):
                load(q, u).wait()

    def update(tile, start, stop):
        for q in range(1, rb):
            @pl.loop(start, stop)
            def _(j):
                acc[q, tile] -= jnp.dot(
                    lower[q, j], natural[j, tile], preferred_element_type=jnp.float32
                )

    @pl.loop(0, steps * chunks)
    def _(e):
        inner = e % (2 * chunks)
        k_plain, t_plain = e // chunks, e % chunks
        middle = inner - ahead
        head = inner < ahead
        tail = inner >= 2 * chunks - ahead
        own = head | (jnp.logical_not(tail) & (middle % 2 == 0))
        k_pair = 2 * (e // (2 * chunks)) + jnp.where(own, 1, 0)
        t_pair = jnp.where(
            head,
            inner,
            jnp.where(
                tail,
                inner - chunks,
                jnp.where(own, ahead + middle // 2, middle // 2),
            ),
        )
        k = k_plain + side * (k_pair - k_plain)
        t = t_plain + side * (t_pair - t_plain)

        @pl.when((e == mine * chunks) & (mine >= 1) & (side == 0))
        def _():
            @pl.loop(jnp.where(early, half, 0), chunks)
            def _(p):
                send_piece(p)

        begin = (mine + 1) * chunks
        late = (mine >= 1) & (side == 1) & (mine < steps - 1)

        @pl.when(late & jnp.logical_not(early) & (e == begin))
        def _():
            @pl.loop(0, half)
            def _(p):
                send_piece(p)

        @pl.when(late & (e > begin) & (e <= begin + chunks - half))
        def _():
            send_piece(e - begin - 1 + half)

        @pl.when((e == gather_at) & ((mine < 0) | (side == 0)))
        def _():
            gather()

            @pl.loop(0, tiles)
            def _(u):
                update(u, 0, last)

        @pl.when(mine != k)
        def _():
            for p in range(2):
                send_low(0, k, t, p).wait_recv()
                forward_half(k, t, p)

            @pl.when(t % fold == fold - 1)
            def _():
                unpack(k, t // fold)

        @pl.when((side == 1) & (k % 2 == 0) & (k + 3 <= mine) & (t % fold == fold - 1))
        def _():
            @pl.when((k == 0) & (t == fold - 1))
            def _():
                receive_blocks(0, inv_index)

            @pl.loop(k, k + 2)
            def _(j):
                acc[0, t // fold] -= jnp.dot(
                    lower[0, j], natural[j, t // fold], preferred_element_type=jnp.float32
                )

        @pl.when(mine == k + 1)
        def _():
            @pl.when((t == 0) & ((side == 0) | (mine == 1)))
            def _():
                receive_blocks(0, inv_index)

            produce(t)

            @pl.when((mine == steps - 1) & (jnp.logical_not(early) | (t >= half)))
            def _():
                send_piece(t)

        @pl.when((k == last) & (t % fold == fold - 1) & ((mine < 0) | (side == 0)))
        def _():
            tile = t // fold
            update(tile, last, steps)
            for q in range(1, rb):
                store_rem(q, tile).start()

    @pl.when((mine >= 0) & (side == 1))
    def _():
        gather()

        @pl.loop(0, tiles)
        def _(u):
            update(u, 0, steps)
            for q in range(1, rb):
                store_rem(q, u).start()

    for k in range(steps):
        for way in range(3):
            @pl.when(goes(way, k))
            def _():
                pltpu.make_async_remote_copy(
                    src_ref=low.at[k], dst_ref=low.at[k],
                    send_sem=send_sem.at[way, k], recv_sem=recv_sem.at[k, 0, 0],
                    device_id={"row": targets[way]}, device_id_type=MESH,
                ).wait_send()
    for q in range(rb):
        for j in range(n_cols):
            used = mine > j if q == 0 else mine >= -n_rows
            for b in range(len(bits)):
                @pl.when(used & passes(j, b))
                def _():
                    send_block(q, j, b).wait_send()
    for k in range(steps):
        pltpu.make_async_copy(natural.at[k], natural.at[k], low_sem.at[k]).wait()
    for q in range(rb):
        pltpu.make_async_copy(acc.at[q], acc.at[q], rem_sem.at[q]).wait()


def on_device(n_rows, n_cols, panel, rhs, inverse):
    rb, block = panel.shape[0], panel.shape[2]
    cols = rhs.shape[3]
    steps = inverse.shape[0]
    assert panel.shape[3] == 1 and n_cols == steps
    assert n_rows % 2 == 0 and steps % 2 == 0 and n_cols & (n_cols - 1) == 0
    width = 128 if cols % 128 == 0 else cols
    tiles = cols // width
    fold = 2
    bits = n_cols.bit_length() - 1
    dma = pltpu.SemaphoreType.DMA
    low, remainder = pl.pallas_call(
        functools.partial(kernel, n_rows, n_cols, steps),
        out_shape=(
            jax.ShapeDtypeStruct((steps, block, cols), jnp.bfloat16),
            jax.ShapeDtypeStruct((rb, block, cols), jnp.float32),
        ),
        in_specs=[pl.BlockSpec(memory_space=pltpu.HBM)] * 3,
        out_specs=(pl.BlockSpec(memory_space=pl.ANY),) * 2,
        scratch_shapes=[
            pltpu.VMEM((steps, tiles * fold, block // fold, width), jnp.bfloat16),
            pltpu.VMEM((steps, tiles, block, width), jnp.bfloat16),
            pltpu.VMEM((rb, tiles, block, width), jnp.float32),
            pltpu.VMEM((block, block), jnp.bfloat16),
            pltpu.VMEM((rb, steps, block, block), jnp.bfloat16),
            dma((rb, tiles)),
            dma((rb,)),
            dma,
            dma((steps,)),
            dma((rb,)),
            dma((3, steps)),
            dma((steps, tiles * fold, 2)),
            dma((rb, n_cols, bits)),
            dma((rb, n_cols)),
        ],
        compiler_params=pltpu.CompilerParams(
            collective_id=0, has_side_effects=True, vmem_limit_bytes=40 * 2**20
        ),
    )(*(
        pltpu.with_memory_space_constraint(x, pltpu.HBM)
        for x in (panel.reshape(rb, block, block), rhs.reshape(rb, block, cols), inverse)
    ))
    return low.astype(jnp.float32), remainder.reshape(rhs.shape)


def solution(mesh):
    placed = (P(None, "row", None, "col", None), P(None, "row", None, "col"), P())
    return jax.shard_map(
        functools.partial(on_device, mesh.shape["row"], mesh.shape["col"]),
        mesh=mesh,
        in_specs=placed,
        out_specs=(P(None, None, "col"), P(None, "row", None, "col")),
        check_vma=False,
    )
```

```python
import functools

import jax
import jax.numpy as jnp
from jax import lax
from jax.experimental import pallas as pl
from jax.experimental.pallas import tpu as pltpu
from jax.sharding import PartitionSpec as P

MESH = pl.DeviceIdType.MESH


def kernel(
    n_rows, n_cols, steps, panel, rhs, inverse, low_out, rem_out,
    low, natural, acc, inv, lower,
    load_sem, own_sem, inv_sem, low_sem, rem_sem, send_sem, recv_sem, psend_sem, precv_sem,
):
    rb = acc.shape[0]
    tiles, block, width = acc.shape[1:]
    chunks = low.shape[1]
    fold = chunks // tiles
    part, height = width // fold, block // fold
    offset = n_rows - steps
    levels = n_rows // 2
    bits = [1 << b for b in reversed(range(n_cols.bit_length() - 1))]
    row, col = lax.axis_index("row"), lax.axis_index("col")
    level, side = row // 2, row % 2
    mine = row - offset
    inv_index = jnp.maximum(mine, 0)

    def flip(bit):
        return col + bit - 2 * bit * ((col // bit) % 2)

    targets = (row + 1 - 2 * side, row - 2, row + 2)
    exists = (level >= 0, level > 0, level < levels - 1)

    def columns(t):
        return pl.ds(pl.multiple_of(t * width, width), width)

    def load(q, t):
        return pltpu.make_async_copy(rhs.at[q, :, columns(t)], acc.at[q, t], load_sem.at[q, t])

    def load_own(q):
        return pltpu.make_async_copy(panel.at[q], lower.at[q, col], own_sem.at[q])

    load_inv = pltpu.make_async_copy(inverse.at[inv_index], inv, inv_sem)

    def store_low(k, t):
        return pltpu.make_async_copy(natural.at[k, t], low_out.at[k, :, columns(t)], low_sem.at[k])

    def store_rem(q, t):
        return pltpu.make_async_copy(acc.at[q, t], rem_out.at[q, :, columns(t)], rem_sem.at[q])

    def send_low(way, k, t, p):
        rows = pl.ds(p * (height // 2), height // 2)
        return pltpu.make_async_remote_copy(
            src_ref=low.at[k, t, rows], dst_ref=low.at[k, t, rows],
            send_sem=send_sem.at[way, k], recv_sem=recv_sem.at[k, t, p],
            device_id={"row": targets[way]}, device_id_type=MESH,
        )

    def goes(way, k):
        home = (offset + k) // 2
        same = k % 2 == side
        if way == 0:
            return same
        if way == 1:
            return same & (level > 0) & (level <= home)
        return same & (level < levels - 1) & (level >= home)

    def forward(k, t):
        for p in range(2):
            forward_half(k, t, p)

    def forward_half(k, t, p):
        for way, when in ((0, side == 0), (2, True), (1, True), (0, side == 1)):
            @pl.when(goes(way, k) & when)
            def _():
                send_low(way, k, t, p).start()

    lane = lax.broadcasted_iota(jnp.int32, (height, width), 1) // part

    def turn(x, shift):
        return pltpu.roll(x, lax.rem(shift + width, width), 1)

    def spread(p):
        wide = p.astype(jnp.float32)
        return jnp.concatenate(
            [wide] + [pltpu.roll(wide, width - g * part, 1) for g in range(1, fold)], axis=0
        ).astype(jnp.bfloat16)

    def pack(x):
        out = x[:height]
        for g in range(1, fold):
            moved = pltpu.roll(x[g * height : (g + 1) * height], g * part, 1)
            out = jnp.where(lane == g, moved, out)
        return out.astype(jnp.bfloat16)

    def unpack(k, tile):
        held = [low[k, tile * fold + h].astype(jnp.float32) for h in range(fold)]
        for g in range(fold):
            out = held[0] if g == 0 else pltpu.roll(held[0], width - g * part, 1)
            for h in range(1, fold):
                shift = (h - g) * part % width
                moved = held[h] if shift == 0 else pltpu.roll(held[h], shift, 1)
                out = jnp.where(lane == h, moved, out)
            natural[k, tile, pl.ds(g * height, height), :] = out.astype(jnp.bfloat16)
        store_low(k, tile).start()

    def send_block(q, j, b):
        return pltpu.make_async_remote_copy(
            src_ref=lower.at[q, j], dst_ref=lower.at[q, j],
            send_sem=psend_sem.at[q, j, b], recv_sem=precv_sem.at[q, j],
            device_id={"col": flip(bits[b])}, device_id_type=MESH,
        )

    def send_own(q):
        load_own(q).wait()
        for b in reversed(range(len(bits))):
            send_block(q, col, b).start()

    def send_piece(p):
        rows = pl.ds(pl.multiple_of(p * (block // chunks), block // chunks), block // chunks)
        for q in range(1, rb):
            @pl.when(p == 0)
            def _():
                load_own(q).wait()

            for b in reversed(range(len(bits))):
                pltpu.make_async_remote_copy(
                    src_ref=lower.at[q, col, rows], dst_ref=lower.at[q, col, rows],
                    send_sem=psend_sem.at[q, col, b], recv_sem=precv_sem.at[q, col],
                    device_id={"col": flip(bits[b])}, device_id_type=MESH,
                ).start()

    def passes(j, b):
        return (col % (2 * bits[b])) == (j % (2 * bits[b]))

    def receive_blocks(q, count):
        def duty(j):
            return (col != j) & passes(j, len(bits) - 1)

        @pl.loop(0, count)
        def _(j):
            @pl.when(duty(j))
            def _():
                send_block(q, j, 0).wait_recv()
                for b in reversed(range(len(bits))):
                    @pl.when(passes(j, b))
                    def _():
                        send_block(q, j, b).start()

        @pl.loop(0, count)
        def _(j):
            @pl.when((col != j) & jnp.logical_not(duty(j)))
            def _():
                send_block(q, j, 0).wait_recv()

    @pl.when(mine >= 0)
    def _():
        load_inv.start()

    @pl.loop(0, tiles)
    def _(t):
        load(0, t).start()

    for q in range(rb):
        load_own(q).start()
    for q in range(1, rb):
        @pl.loop(0, tiles)
        def _(t):
            load(q, t).start()

    barrier = pltpu.get_barrier_semaphore()
    for way in range(3):
        @pl.when(exists[way])
        def _():
            pl.semaphore_signal(barrier, inc=1, device_id={"row": targets[way]}, device_id_type=MESH)
    for bit in bits:
        pl.semaphore_signal(barrier, inc=1, device_id={"col": flip(bit)}, device_id_type=MESH)
    def solve_first(t):
        load(0, t).wait()
        fresh = jnp.dot(
            inv[...], acc[0, t].astype(jnp.bfloat16), preferred_element_type=jnp.float32
        )
        natural[0, t] = fresh.astype(jnp.bfloat16)
        for h in range(fold):
            low[0, t * fold + h] = pack(
                fresh if h == 0 else pltpu.roll(fresh, width - h * part, 1)
            )

    @pl.when(mine == 0)
    def _():
        load_inv.wait()
        solve_first(0)

    pl.semaphore_wait(
        barrier,
        1 + len(bits) + jnp.minimum(level, 1) + jnp.minimum(levels - 1 - level, 1),
    )

    @pl.when(mine == 0)
    def _():
        @pl.loop(0, tiles)
        def _(t):
            @pl.when(t > 0)
            def _():
                solve_first(t)

            for h in range(fold):
                forward(0, t * fold + h)
            store_low(0, t).start()
            store_rem(0, t).start()

    @pl.when((mine > col) & (mine != 1))
    def _():
        send_own(0)

    @pl.when((mine > col) & (mine == 1))
    def _():
        load_own(0).wait()
        for b in range(len(bits)):
            send_block(0, col, b).start()

    @pl.when(mine <= col)
    def _():
        load_own(0).wait()

    def send_later():
        for q in range(1, rb):
            send_own(q)

    @pl.when(mine <= 0)
    def _():
        send_later()

    early = (mine >= 1) & (col >= mine) & (col >= n_cols // 2)
    half = chunks // 2

    @pl.when(early)
    def _():
        @pl.loop(0, half)
        def _(p):
            send_piece(p)

    @pl.when(mine != 0)
    def _():
        @pl.loop(0, tiles)
        def _(t):
            load(0, t).wait()

    def produce(t):
        tile, h = t // fold, t % fold

        @pl.when((h == 0) & (side == 0))
        def _():
            @pl.loop(0, inv_index - 1)
            def _(j):
                acc[0, tile] -= jnp.dot(
                    lower[0, j], natural[j, tile], preferred_element_type=jnp.float32
                )

        base = turn(acc[0, tile], -h * part)
        prev = inv_index - 1
        base = base - jnp.dot(
            lower[0, prev], spread(low[prev, t]), preferred_element_type=jnp.float32
        )
        low[inv_index, t] = pack(
            jnp.dot(inv[...], base.astype(jnp.bfloat16), preferred_element_type=jnp.float32)
        )
        forward(inv_index, t)
        group = lax.broadcasted_iota(jnp.int32, (block, width), 1) // part
        acc[0, tile] = jnp.where(group == h, turn(base, h * part), acc[0, tile])

        @pl.when(h == fold - 1)
        def _():
            store_rem(0, tile).start()
            unpack(inv_index, tile)

    @pl.when(mine >= 1)
    def _():
        load_inv.wait()

    @pl.when(mine < 0)
    def _():
        @pl.loop(0, tiles)
        def _(t):
            store_rem(0, t).start()

    last = steps - 1 - side
    gather_at = last * chunks

    def gather():
        for q in range(1, rb):
            receive_blocks(q, n_cols)

            @pl.loop(0, tiles)
            def _(u):
                load(q, u).wait()

    def update(tile, start, stop):
        for q in range(1, rb):
            @pl.loop(start, stop)
            def _(j):
                acc[q, tile] -= jnp.dot(
                    lower[q, j], natural[j, tile], preferred_element_type=jnp.float32
                )

    @pl.loop(0, steps * chunks)
    def _(e):
        inner = e % (2 * chunks)
        k_plain, t_plain = e // chunks, e % chunks
        k_pair, t_pair = 2 * (e // (2 * chunks)) + 1 - inner % 2, inner // 2
        k = k_plain + side * (k_pair - k_plain)
        t = t_plain + side * (t_pair - t_plain)

        @pl.when((e == mine * chunks) & (mine >= 1) & (side == 0))
        def _():
            @pl.loop(jnp.where(early, half, 0), chunks)
            def _(p):
                send_piece(p)

        begin = (mine + 1) * chunks
        late = (mine >= 1) & (side == 1) & (mine < steps - 1)

        @pl.when(late & jnp.logical_not(early) & (e == begin))
        def _():
            @pl.loop(0, half)
            def _(p):
                send_piece(p)

        @pl.when(late & (e > begin) & (e <= begin + chunks - half))
        def _():
            send_piece(e - begin - 1 + half)

        @pl.when((e == gather_at) & ((mine < 0) | (side == 0)))
        def _():
            gather()

            @pl.loop(0, tiles)
            def _(u):
                update(u, 0, last)

        @pl.when(mine != k)
        def _():
            for p in range(2):
                send_low(0, k, t, p).wait_recv()
                forward_half(k, t, p)

            @pl.when(t % fold == fold - 1)
            def _():
                unpack(k, t // fold)

        @pl.when((side == 1) & (k % 2 == 0) & (k + 3 <= mine) & (t % fold == fold - 1))
        def _():
            @pl.when((k == 0) & (t == fold - 1))
            def _():
                receive_blocks(0, inv_index)

            @pl.loop(k, k + 2)
            def _(j):
                acc[0, t // fold] -= jnp.dot(
                    lower[0, j], natural[j, t // fold], preferred_element_type=jnp.float32
                )

        @pl.when(mine == k + 1)
        def _():
            @pl.when((t == 0) & ((side == 0) | (mine == 1)))
            def _():
                receive_blocks(0, inv_index)

            produce(t)

            @pl.when((mine == steps - 1) & (jnp.logical_not(early) | (t >= half)))
            def _():
                send_piece(t)

        @pl.when((k == last) & (t % fold == fold - 1) & ((mine < 0) | (side == 0)))
        def _():
            tile = t // fold
            update(tile, last, steps)
            for q in range(1, rb):
                store_rem(q, tile).start()

    @pl.when((mine >= 0) & (side == 1))
    def _():
        gather()

        @pl.loop(0, tiles)
        def _(u):
            update(u, 0, steps)
            for q in range(1, rb):
                store_rem(q, u).start()

    for k in range(steps):
        for way in range(3):
            @pl.when(goes(way, k))
            def _():
                pltpu.make_async_remote_copy(
                    src_ref=low.at[k], dst_ref=low.at[k],
                    send_sem=send_sem.at[way, k], recv_sem=recv_sem.at[k, 0, 0],
                    device_id={"row": targets[way]}, device_id_type=MESH,
                ).wait_send()
    for q in range(rb):
        for j in range(n_cols):
            used = mine > j if q == 0 else mine >= -n_rows
            for b in range(len(bits)):
                @pl.when(used & passes(j, b))
                def _():
                    send_block(q, j, b).wait_send()
    for k in range(steps):
        pltpu.make_async_copy(natural.at[k], natural.at[k], low_sem.at[k]).wait()
    for q in range(rb):
        pltpu.make_async_copy(acc.at[q], acc.at[q], rem_sem.at[q]).wait()


def on_device(n_rows, n_cols, panel, rhs, inverse):
    rb, block = panel.shape[0], panel.shape[2]
    cols = rhs.shape[3]
    steps = inverse.shape[0]
    assert panel.shape[3] == 1 and n_cols == steps
    assert n_rows % 2 == 0 and steps % 2 == 0 and n_cols & (n_cols - 1) == 0
    width = 128 if cols % 128 == 0 else cols
    tiles = cols // width
    fold = 2
    bits = n_cols.bit_length() - 1
    dma = pltpu.SemaphoreType.DMA
    low, remainder = pl.pallas_call(
        functools.partial(kernel, n_rows, n_cols, steps),
        out_shape=(
            jax.ShapeDtypeStruct((steps, block, cols), jnp.bfloat16),
            jax.ShapeDtypeStruct((rb, block, cols), jnp.float32),
        ),
        in_specs=[pl.BlockSpec(memory_space=pltpu.HBM)] * 3,
        out_specs=(pl.BlockSpec(memory_space=pl.ANY),) * 2,
        scratch_shapes=[
            pltpu.VMEM((steps, tiles * fold, block // fold, width), jnp.bfloat16),
            pltpu.VMEM((steps, tiles, block, width), jnp.bfloat16),
            pltpu.VMEM((rb, tiles, block, width), jnp.float32),
            pltpu.VMEM((block, block), jnp.bfloat16),
            pltpu.VMEM((rb, steps, block, block), jnp.bfloat16),
            dma((rb, tiles)),
            dma((rb,)),
            dma,
            dma((steps,)),
            dma((rb,)),
            dma((3, steps)),
            dma((steps, tiles * fold, 2)),
            dma((rb, n_cols, bits)),
            dma((rb, n_cols)),
        ],
        compiler_params=pltpu.CompilerParams(
            collective_id=0, has_side_effects=True, vmem_limit_bytes=40 * 2**20
        ),
    )(*(
        pltpu.with_memory_space_constraint(x, pltpu.HBM)
        for x in (panel.reshape(rb, block, block), rhs.reshape(rb, block, cols), inverse)
    ))
    return low.astype(jnp.float32), remainder.reshape(rhs.shape)


def solution(mesh):
    placed = (P(None, "row", None, "col", None), P(None, "row", None, "col"), P())
    return jax.shard_map(
        functools.partial(on_device, mesh.shape["row"], mesh.shape["col"]),
        mesh=mesh,
        in_specs=placed,
        out_specs=(P(None, None, "col"), P(None, "row", None, "col")),
        check_vma=False,
    )
```
